512 devices in a mesh: blk: 64 (over y, z_hi, core), head: 8 (over z_lo, x).
Axes of the slice: x: 4, y: 8, z: 8 (z_hi: 4, z_lo: 2; z = z_hi * 2 + z_lo), core: 2. Of those that a mesh axis runs over, the one named last changes fastest.
Arguments:
- query_nope: bfloat16 [4096, 8192], P('blk', 'head'), may hold values from -140 to 140
- query_rope: bfloat16 [4096, 4096], P('blk', 'head'), may hold values from -6 to 6
- compressed: bfloat16 [4096, 576], P(('blk', 'head')), may hold values from -6 to 6
- latent_gain: float32 [512], replicated, may hold values from 0.1 to 1.9
- key_up: bfloat16 [64, 128, 512], P('head'), may hold values from -0.5 to 0.5
- value_up: bfloat16 [64, 512, 128], P('head'), may hold values from -1.5 to 1.5
- span_order: int32 [128], replicated, may hold values from 0 to 127, each once
Outputs:
- attended: bfloat16 [4096, 8192], P('blk', 'head')
The draws below stay inside these ranges and needn't reach their ends.
Inputs may be any that keep to these rules, and one draw needn't show every extreme that they name: Every number appears once; device index i of blk holds the blocks span_order[2 i] and span_order[2 i + 1].
All inputs are finite; a program needn't handle non-finite values.
Results may differ from the reference program's by a relative error of at most 0.0075.
The reference program's roundings to bfloat16 on the way count: a program that leaves them out, or rounds other values in their place, can miss the bound.
Values may be sent and summed in bfloat16 or wider, within the bound.
No kernel may reach another device: no remote copies, remote signals or barrier semaphores. Data moves between devices by JAX's collectives and lax.ppermute only.
A program may use at most 64 MiB of HBM per device.

```python
import jax
import jax.numpy as jnp
from jax import lax

LATENT = 512
ROPE = 64
NOPE = 128
VDIM = 128
HEADS = 64
TOK_DEV = 64
TOKENS = 4096
N_BLK = 64


def draw_query_nope(key, part):
    first_key = jax.random.fold_in(jax.random.fold_in(key, 17), 0)
    values = jax.random.truncated_normal(first_key, -6.0, 6.0, (TOKENS, HEADS, NOPE), jnp.float32)
    return values.reshape(TOKENS, HEADS * NOPE).astype(jnp.bfloat16)


def block_levels(rng, dims, cuts, low, high):
    def one(position, blocks):
        steps = jax.random.uniform(jax.random.fold_in(jax.random.fold_in(rng, 6), position), (blocks,), jnp.float32, low / len(cuts), high / len(cuts))
        return jnp.repeat(jnp.exp(steps), dims[position] // blocks).reshape((-1,) + (1,) * (len(dims) - position - 1))

    loudness = one(*cuts[0])
    for cut in cuts[1:]:
        loudness = loudness * one(*cut)
    return loudness


def normal_values(own_key, shape, width, limit, cuts=(), kind=jnp.bfloat16):
    factor_of = block_levels(own_key, shape, cuts, -0.22, 0.18) if cuts else 1.0
    drawn = jax.random.normal(own_key, shape, jnp.float32) * width * factor_of
    return jnp.minimum(jnp.maximum(drawn, -limit), limit).astype(kind)


def setup_inputs(seed: int = 0) -> dict:
    arg_keys = jax.random.split(jax.random.key(seed), 8)
    return {
        "query_nope": draw_query_nope(jax.random.fold_in(arg_keys[7], 71), 0),
        "query_rope": normal_values(arg_keys[1], (TOKENS, HEADS * ROPE), 1.0, 6.0, ((0, 64), (1, 8))),
        "compressed": normal_values(arg_keys[2], (TOKENS, LATENT + ROPE), 1.0, 6.0, ((0, 512),)),
        "latent_gain": jnp.clip(1.0 + 0.18 * jax.random.normal(arg_keys[3], (LATENT,), jnp.float32), 0.1, 1.9),
        "key_up": normal_values(arg_keys[4], (HEADS, NOPE, LATENT), NOPE ** -0.5, 0.5, ((0, 8),)),
        "value_up": normal_values(arg_keys[5], (HEADS, LATENT, VDIM), (LATENT // 32) ** -0.5, 1.5, ((0, 8),)),
        "span_order": jax.random.permutation(arg_keys[6], 2 * N_BLK).astype(jnp.int32),
    }


norm_epsilon = 1e-06
rope_base = 10000.0
masked_score = -1e+30

def lookup(entries, index_array):
    slots = jnp.arange(entries.shape[0], dtype=jnp.int32)
    matches = index_array[..., None] == slots
    return lax.optimization_barrier(jnp.sum(jnp.where(matches, entries, 0), axis=-1)).astype(jnp.int32)

def rotate(values, positions):
    half_width = values.shape[-1] // 2
    frequency = rope_base ** (-jnp.arange(half_width, dtype=jnp.float32) / half_width)
    angles = positions.astype(jnp.float32)[..., None] * frequency
    cosine = jnp.cos(angles)
    sine_value = jnp.sin(angles)
    leading = values[..., :half_width]
    trailing = values[..., half_width:]
    return jnp.concatenate([leading * cosine - trailing * sine_value, leading * sine_value + trailing * cosine], axis=-1)

def reference(query_nope, query_rope, compressed, latent_gain, key_up, value_up, span_order):
    half_block = TOK_DEV // 2
    row_ids = jnp.arange(TOKENS, dtype=jnp.int32)
    positions = lookup(span_order, row_ids // half_block) * half_block + row_ids % half_block
    latent = compressed[:, :LATENT].astype(jnp.float32)
    latent = latent * lax.rsqrt(lax.optimization_barrier(jnp.mean(latent * latent, axis=1, keepdims=True)) + norm_epsilon) * latent_gain
    latent = latent.astype(jnp.bfloat16)
    key_rot = rotate(compressed[:, LATENT:].astype(jnp.float32), positions).astype(jnp.bfloat16)
    key_matrix = jnp.concatenate([latent, key_rot], axis=1)
    nope_parts = query_nope.reshape(TOKENS, HEADS, NOPE)
    query_rot = rotate(query_rope.reshape(TOKENS, HEADS, ROPE).astype(jnp.float32), positions[:, None]).astype(jnp.bfloat16)
    visible = positions[None, :] <= positions[:, None]
    score_scale = (NOPE + ROPE) ** (-0.5)

    def one_head(head_index):
        query_lat = jnp.dot(nope_parts[:, head_index, :], key_up[head_index], preferred_element_type=jnp.float32).astype(jnp.bfloat16)
        queries = jnp.concatenate([query_lat, query_rot[:, head_index, :]], axis=1)
        scores = jnp.dot(queries, key_matrix.T, preferred_element_type=jnp.float32) * score_scale
        scores = jnp.where(visible, scores, masked_score)
        row_max = lax.optimization_barrier(jnp.max(scores, axis=1, keepdims=True))
        weight = jnp.where(visible, jnp.exp(scores - row_max), 0.0)
        totals = lax.optimization_barrier(jnp.sum(weight, axis=1, keepdims=True))
        lat_out = jnp.dot(weight.astype(jnp.bfloat16), latent, preferred_element_type=jnp.float32) / totals
        lat_out = lat_out.astype(jnp.bfloat16)
        return jnp.dot(lat_out, value_up[head_index], preferred_element_type=jnp.float32).astype(jnp.bfloat16)
    outputs = lax.map(one_head, jnp.arange(HEADS, dtype=jnp.int32))
    return jnp.transpose(outputs, (1, 0, 2)).reshape(TOKENS, HEADS * VDIM)
```

```python
import functools

import jax
import jax.numpy as jnp
import numpy as np
from jax import lax
from jax.experimental import pallas as pl
from jax.experimental.pallas import tpu as pltpu
from jax.sharding import Mesh
from jax.sharding import PartitionSpec as P

AXES = ("y", "zh", "c", "zl", "x")
BLK = ("y", "zh", "c")
HEAD = ("zl", "x")
PLANE = ("y", "zh", "zl")
NY, NZH, NC, NZL, NX = 8, 4, 2, 2, 4

LATENT = 512
ROPE = 64
NOPE = 128
VDIM = 128
HEADS_HERE = 8
TOK = 64
HALF = 32
WIDE = 640
ROWS = TOK * HEADS_HERE
CHUNK = 256

norm_epsilon = 1e-06
rope_base = 10000.0
masked_score = -1e30
score_scale = (NOPE + ROPE) ** (-0.5)
log2e = 1.4426950408889634

FREQUENCY = np.tile(
    np.float32(rope_base) ** (-np.arange(ROPE // 2, dtype=np.float32) / np.float32(ROPE // 2)),
    128 // (ROPE // 2),
).astype(np.float32)[None]

VMEM = pl.BlockSpec(memory_space=pltpu.VMEM)
SMEM = pl.BlockSpec(memory_space=pltpu.SMEM)


def lanes_of(shape):
    return lax.broadcasted_iota(jnp.int32, shape, 1)


def rotated(values, positions, frequency):
    lane = lanes_of(values.shape)
    leading = lane % ROPE < ROPE // 2
    angles = positions * frequency
    cosine = jnp.cos(angles)
    sine_value = jnp.where(leading, -jnp.sin(angles), jnp.sin(angles))
    return cosine, sine_value, leading


def apply_rotation(values, cosine, sine_value, leading):
    swapped = jnp.where(
        leading,
        pltpu.roll(values, 128 - ROPE // 2, 1),
        pltpu.roll(values, ROPE // 2, 1),
    )
    return values * cosine + swapped * sine_value


def block_index():
    return (lax.axis_index("y") * NZH + lax.axis_index("zh")) * NC + lax.axis_index("c")


def prep_kernel(span_ref, compressed_ref, gain_ref, frequency_ref, out_ref):
    rows = compressed_ref.shape[0]
    block = block_index()
    x = lax.axis_index("x")
    span = span_ref[block * 2 + lax.axis_index("zl")]
    offset = x * rows + lax.broadcasted_iota(jnp.int32, (rows, 128), 0)
    latent = compressed_ref[:, :LATENT].astype(jnp.float32)
    scale = lax.rsqrt(jnp.mean(latent * latent, axis=1, keepdims=True) + norm_epsilon)
    latent = (latent * scale * gain_ref[...]).astype(jnp.bfloat16)
    rope = compressed_ref[:, LATENT:].astype(jnp.float32)
    rope = jnp.concatenate([rope, jnp.zeros_like(rope)], axis=1)
    positions = (span * HALF + offset).astype(jnp.float32)
    cosine, sine_value, leading = rotated(rope, positions, frequency_ref[...])
    turned = apply_rotation(rope, cosine, sine_value, leading)
    lane = lanes_of((rows, 128))
    tail = jnp.where(
        lane < ROPE,
        turned,
        jnp.where(
            lane == ROPE,
            span.astype(jnp.float32),
            jnp.where(lane == ROPE + 1, offset.astype(jnp.float32), 0.0),
        ),
    ).astype(jnp.bfloat16)
    row = jnp.concatenate([latent, tail], axis=1)
    out_ref[...] = jnp.broadcast_to(row[None], out_ref.shape)


def key_positions(keys):
    lane = lanes_of((16, WIDE))
    pick = jnp.where(
        lane == LATENT + ROPE, float(HALF), jnp.where(lane == LATENT + ROPE + 1, 1.0, 0.0)
    ).astype(jnp.bfloat16)
    found = lax.dot_general(
        pick, keys, (((1,), (1,)), ((), ())), preferred_element_type=jnp.float32
    )
    return found[:1]


def query_positions(span_ref, start, count):
    block = block_index()
    other = start // ROWS
    block = block + other * (1 - 2 * lax.axis_index("c"))
    row = lax.broadcasted_iota(jnp.int32, (count, 1), 0)
    first = span_ref[block * 2] * HALF
    second = span_ref[block * 2 + 1] * HALF
    token = row % TOK
    return jnp.where(token < HALF, first + token, second + token - HALF).astype(jnp.float32)


def attend(span_ref, query_ref, key_refs, carry, finish):
    keys = [ref[...] for ref in key_refs]
    places = [key_positions(block) for block in keys]
    for start in range(0, 2 * ROWS, CHUNK):
        queries = query_ref[start : start + CHUNK, :]
        here = query_positions(span_ref, start, CHUNK)
        scores = []
        for block, place in zip(keys, places):
            raw = lax.dot_general(
                queries, block, (((1,), (1,)), ((), ())), preferred_element_type=jnp.float32
            )
            scores.append(jnp.where(place <= here, raw * (score_scale * log2e), masked_score))
        tops = [jnp.max(score, axis=1, keepdims=True) for score in scores]
        top = functools.reduce(jnp.maximum, tops)
        if carry is not None:
            old_acc, old_top, old_sum = carry
            before = old_top[start : start + CHUNK, :1]
            top = jnp.maximum(top, before)
        product = None
        total = None
        for block, score in zip(keys, scores):
            weight = jnp.exp2(score - top)
            for at in range(0, weight.shape[1], 128):
                part = weight[:, at : at + 128]
                total = part if total is None else total + part
            term = jnp.dot(
                weight.astype(jnp.bfloat16), block[:, :LATENT], preferred_element_type=jnp.float32
            )
            product = term if product is None else product + term
        if carry is not None:
            shrink = jnp.exp2(before - top)
            product = product + old_acc[start : start + CHUNK, :] * shrink
            total = total + old_sum[start : start + CHUNK, :] * shrink
        finish(start, product, top, total)


def first_kernel(
    span_ref,
    frequency_ref,
    nope_ref,
    rope_ref,
    sibling_ref,
    key_up_ref,
    keys_ref,
    query_ref,
    acc_ref,
    top_ref,
    sum_ref,
):
    for other in range(2):
        if other == 0:
            nope = nope_ref[...]
            rope = rope_ref[...]
        else:
            nope = sibling_ref[:, : HEADS_HERE * NOPE]
            rope = sibling_ref[:, HEADS_HERE * NOPE :]
        base = other * ROWS
        positions = jnp.broadcast_to(query_positions(span_ref, base, TOK), (TOK, 128))
        cosine, sine_value, leading = rotated(positions, positions, frequency_ref[...])
        lane = lanes_of((TOK, 128))
        for head in range(HEADS_HERE):
            at = base + head * TOK
            query_ref[at : at + TOK, :LATENT] = jnp.dot(
                nope[:, head * NOPE : (head + 1) * NOPE],
                key_up_ref[head],
                preferred_element_type=jnp.float32,
            ).astype(jnp.bfloat16)
        for pair in range(HEADS_HERE // 2):
            turned = apply_rotation(
                rope[:, pair * 128 : (pair + 1) * 128].astype(jnp.float32),
                cosine,
                sine_value,
                leading,
            )
            for side in range(2):
                at = base + (pair * 2 + side) * TOK
                shifted = turned if side == 0 else pltpu.roll(turned, ROPE, 1)
                query_ref[at : at + TOK, LATENT:] = jnp.where(lane < ROPE, shifted, 0.0).astype(
                    jnp.bfloat16
                )

    def finish(start, product, top, total):
        acc_ref[start : start + CHUNK, :] = product
        top_ref[start : start + CHUNK, :] = jnp.broadcast_to(top, (CHUNK, 128))
        sum_ref[start : start + CHUNK, :] = total

    attend(span_ref, query_ref, [keys_ref], None, finish)


def middle_kernel(
    span_ref,
    query_ref,
    one_ref,
    two_ref,
    old_acc_ref,
    old_top_ref,
    old_sum_ref,
    acc_ref,
    top_ref,
    sum_ref,
):
    def finish(start, product, top, total):
        acc_ref[start : start + CHUNK, :] = product
        top_ref[start : start + CHUNK, :] = jnp.broadcast_to(top, (CHUNK, 128))
        sum_ref[start : start + CHUNK, :] = total

    attend(
        span_ref,
        query_ref,
        [one_ref, two_ref],
        (old_acc_ref, old_top_ref, old_sum_ref),
        finish,
    )


def last_kernel(
    span_ref, query_ref, keys_ref, old_acc_ref, old_top_ref, old_sum_ref, own_ref, send_ref
):
    def finish(start, product, top, total):
        ref = own_ref if start < ROWS else send_ref
        at = start % ROWS
        whole = jnp.sum(total, axis=1, keepdims=True)
        lane = lanes_of((CHUNK, 128))
        ref[at : at + CHUNK, :LATENT] = product
        ref[at : at + CHUNK, LATENT:] = jnp.where(lane < 64, top, whole)

    attend(span_ref, query_ref, [keys_ref], (old_acc_ref, old_top_ref, old_sum_ref), finish)


def merge_kernel(own_ref, got_ref, value_up_ref, out_ref):
    for head in range(HEADS_HERE):
        at = slice(head * TOK, (head + 1) * TOK)
        one_top = own_ref[at, LATENT : LATENT + 1]
        two_top = got_ref[at, LATENT : LATENT + 1]
        one_sum = own_ref[at, LATENT + 64 : LATENT + 65]
        two_sum = got_ref[at, LATENT + 64 : LATENT + 65]
        top = jnp.maximum(one_top, two_top)
        one = jnp.exp2(one_top - top)
        two = jnp.exp2(two_top - top)
        total = one_sum * one + two_sum * two
        latent = (own_ref[at, :LATENT] * one + got_ref[at, :LATENT] * two) / total
        out_ref[:, head * VDIM : (head + 1) * VDIM] = jnp.dot(
            latent.astype(jnp.bfloat16), value_up_ref[head], preferred_element_type=jnp.float32
        ).astype(jnp.bfloat16)


def call(kernel, specs, out_shape, name, vmem=32):
    out_specs = jax.tree.map(lambda _: VMEM, out_shape)
    return pl.pallas_call(
        kernel,
        in_specs=specs,
        out_specs=out_specs,
        out_shape=out_shape,
        name=name,
        compiler_params=pltpu.CompilerParams(vmem_limit_bytes=vmem * 1024 * 1024),
    )


def device_at(y, z, x, c):
    y, z, x = y % NY, z % (NZH * NZL), x % NX
    return (((y * NZH + z // NZL) * NC + c) * NZL + z % NZL) * NX + x


def pairs(target):
    return [
        (device_at(y, z, x, c), device_at(*target(y, z, x, c)))
        for y in range(NY)
        for z in range(NZH * NZL)
        for x in range(NX)
        for c in range(NC)
    ]


def shards(query_nope, query_rope, compressed, latent_gain, key_up, value_up, span_order):
    f32 = jnp.float32
    bf16 = jnp.bfloat16
    shape = jax.ShapeDtypeStruct
    frequency = jnp.asarray(FREQUENCY)
    toward = pairs(lambda y, z, x, c: (y, z, x - 1 + 2 * c, c))
    away = pairs(lambda y, z, x, c: (y, z, x + 1 - 2 * c, c))
    across = pairs(lambda y, z, x, c: (y, z, x, 1 - c))

    sent = call(
        prep_kernel, [SMEM, VMEM, VMEM, VMEM], shape((64, 8, WIDE), bf16), "prep", 8
    )(span_order, compressed, latent_gain[None], frequency)
    own_keys = lax.all_to_all(sent, PLANE, 0, 0, tiled=True).reshape(512, WIDE)
    one = lax.ppermute(own_keys, AXES, toward)
    two = lax.ppermute(own_keys, AXES, away)
    sibling = lax.ppermute(jnp.concatenate([query_nope, query_rope], axis=1), AXES, across)
    three = lax.ppermute(one, AXES, toward)
    state = (
        shape((2 * ROWS, LATENT), f32),
        shape((2 * ROWS, 128), f32),
        shape((2 * ROWS, 128), f32),
    )
    queries, *carry = call(
        first_kernel,
        [SMEM] + [VMEM] * 6,
        (shape((2 * ROWS, WIDE), bf16), *state),
        "first",
    )(span_order, frequency, query_nope, query_rope, sibling, key_up, own_keys)
    carry = call(middle_kernel, [SMEM] + [VMEM] * 6, state, "middle")(
        span_order, queries, one, two, *carry
    )
    packet = shape((ROWS, WIDE), f32)
    own, send = call(last_kernel, [SMEM] + [VMEM] * 5, (packet, packet), "last")(
        span_order, queries, three, *carry
    )
    got = lax.ppermute(send, AXES, across)
    return call(
        merge_kernel, [VMEM] * 3, shape((TOK, HEADS_HERE * VDIM), bf16), "merge", 16
    )(own, got, value_up)


def solution(mesh):
    split = Mesh(mesh.devices.reshape(NY, NZH, NC, NZL, NX), AXES)
    placed = (
        P(BLK, HEAD),
        P(BLK, HEAD),
        P(AXES, None),
        P(),
        P(HEAD, None, None),
        P(HEAD, None, None),
        P(),
    )
    return jax.shard_map(
        shards, mesh=split, in_specs=placed, out_specs=P(BLK, HEAD), check_vma=False
    )
```

```python
import functools

import jax
import jax.numpy as jnp
import numpy as np
from jax import lax
from jax.experimental import pallas as pl
from jax.experimental.pallas import tpu as pltpu
from jax.sharding import Mesh
from jax.sharding import PartitionSpec as P

AXES = ("y", "zh", "c", "zl", "x")
BLK = ("y", "zh", "c")
HEAD = ("zl", "x")
PLANE = ("y", "zh", "zl")
NY, NZH, NC, NZL, NX = 8, 4, 2, 2, 4

LATENT = 512
ROPE = 64
NOPE = 128
VDIM = 128
HEADS_HERE = 8
TOK = 64
HALF = 32
WIDE = 640
ROWS = TOK * HEADS_HERE
CHUNK = 256

norm_epsilon = 1e-06
rope_base = 10000.0
masked_score = -1e30
score_scale = (NOPE + ROPE) ** (-0.5)
log2e = 1.4426950408889634

FREQUENCY = np.tile(
    np.float32(rope_base) ** (-np.arange(ROPE // 2, dtype=np.float32) / np.float32(ROPE // 2)),
    128 // (ROPE // 2),
).astype(np.float32)[None]

VMEM = pl.BlockSpec(memory_space=pltpu.VMEM)
SMEM = pl.BlockSpec(memory_space=pltpu.SMEM)
HBM = pl.BlockSpec(memory_space=pltpu.HBM)


def lanes_of(shape):
    return lax.broadcasted_iota(jnp.int32, shape, 1)


def rotated(values, positions, frequency):
    lane = lanes_of(values.shape)
    leading = lane % ROPE < ROPE // 2
    angles = positions * frequency
    cosine = jnp.cos(angles)
    sine_value = jnp.where(leading, -jnp.sin(angles), jnp.sin(angles))
    return cosine, sine_value, leading


def apply_rotation(values, cosine, sine_value, leading):
    swapped = jnp.where(
        leading,
        pltpu.roll(values, 128 - ROPE // 2, 1),
        pltpu.roll(values, ROPE // 2, 1),
    )
    return values * cosine + swapped * sine_value


def block_index():
    return (lax.axis_index("y") * NZH + lax.axis_index("zh")) * NC + lax.axis_index("c")


def prep_kernel(
    span_hbm,
    compressed_hbm,
    gain_hbm,
    frequency_hbm,
    out_ref,
    span_ref,
    compressed_ref,
    gain_ref,
    frequency_ref,
    sems,
):
    copies = [
        pltpu.make_async_copy(source, target, sems.at[k])
        for k, (source, target) in enumerate(
            (
                (compressed_hbm, compressed_ref),
                (gain_hbm, gain_ref),
                (span_hbm, span_ref),
                (frequency_hbm, frequency_ref),
            )
        )
    ]
    for copy in copies:
        copy.start()
    for copy in copies:
        copy.wait()
    rows = compressed_ref.shape[0]
    block = block_index()
    x = lax.axis_index("x")
    span = span_ref[block * 2 + lax.axis_index("zl")]
    offset = x * rows + lax.broadcasted_iota(jnp.int32, (rows, 128), 0)
    latent = compressed_ref[:, :LATENT].astype(jnp.float32)
    scale = lax.rsqrt(jnp.mean(latent * latent, axis=1, keepdims=True) + norm_epsilon)
    latent = (latent * scale * gain_ref[...]).astype(jnp.bfloat16)
    rope = compressed_ref[:, LATENT:].astype(jnp.float32)
    rope = jnp.concatenate([rope, jnp.zeros_like(rope)], axis=1)
    positions = (span * HALF + offset).astype(jnp.float32)
    cosine, sine_value, leading = rotated(rope, positions, frequency_ref[...])
    turned = apply_rotation(rope, cosine, sine_value, leading)
    lane = lanes_of((rows, 128))
    tail = jnp.where(
        lane < ROPE,
        turned,
        jnp.where(
            lane == ROPE,
            span.astype(jnp.float32),
            jnp.where(lane == ROPE + 1, offset.astype(jnp.float32), 0.0),
        ),
    ).astype(jnp.bfloat16)
    row = jnp.concatenate([latent, tail], axis=1)
    out_ref[...] = jnp.broadcast_to(row[None], out_ref.shape)


def key_positions(keys):
    lane = lanes_of((16, WIDE))
    pick = jnp.where(
        lane == LATENT + ROPE, float(HALF), jnp.where(lane == LATENT + ROPE + 1, 1.0, 0.0)
    ).astype(jnp.bfloat16)
    found = lax.dot_general(
        pick, keys, (((1,), (1,)), ((), ())), preferred_element_type=jnp.float32
    )
    return found[:1]


def query_positions(span_ref, start, count):
    block = block_index()
    other = start // ROWS
    block = block + other * (1 - 2 * lax.axis_index("c"))
    row = lax.broadcasted_iota(jnp.int32, (count, 1), 0)
    first = span_ref[block * 2] * HALF
    second = span_ref[block * 2 + 1] * HALF
    token = row % TOK
    return jnp.where(token < HALF, first + token, second + token - HALF).astype(jnp.float32)


def attend(span_ref, query_ref, key_refs, carry, finish, rows=(0, 2 * ROWS)):
    keys = [ref[...] for ref in key_refs]
    places = [key_positions(block) for block in keys]
    for start in range(*rows, CHUNK):
        queries = query_ref[start : start + CHUNK, :]
        here = query_positions(span_ref, start, CHUNK)
        scores = []
        for block, place in zip(keys, places):
            raw = lax.dot_general(
                queries, block, (((1,), (1,)), ((), ())), preferred_element_type=jnp.float32
            )
            scores.append(jnp.where(place <= here, raw * (score_scale * log2e), masked_score))
        tops = [jnp.max(score, axis=1, keepdims=True) for score in scores]
        top = functools.reduce(jnp.maximum, tops)
        if carry is not None:
            old_acc, old_top, old_sum = carry
            before = old_top[start : start + CHUNK, :1]
            top = jnp.maximum(top, before)
        product = None
        total = None
        for block, score in zip(keys, scores):
            weight = jnp.exp2(score - top)
            for at in range(0, weight.shape[1], 128):
                part = weight[:, at : at + 128]
                total = part if total is None else total + part
            term = jnp.dot(
                weight.astype(jnp.bfloat16), block[:, :LATENT], preferred_element_type=jnp.float32
            )
            product = term if product is None else product + term
        if carry is not None:
            shrink = jnp.exp2(before - top)
            product = product + old_acc[start : start + CHUNK, :] * shrink
            total = total + old_sum[start : start + CHUNK, :] * shrink
        finish(start, product, top, total)


def first_kernel(
    span_ref,
    frequency_ref,
    nope_ref,
    rope_ref,
    sibling_ref,
    key_up_ref,
    keys_ref,
    query_ref,
    acc_ref,
    top_ref,
    sum_ref,
):
    for other in range(2):
        if other == 0:
            nope = nope_ref[...]
            rope = rope_ref[...]
        else:
            nope = sibling_ref[:, : HEADS_HERE * NOPE]
            rope = sibling_ref[:, HEADS_HERE * NOPE :]
        base = other * ROWS
        positions = jnp.broadcast_to(query_positions(span_ref, base, TOK), (TOK, 128))
        cosine, sine_value, leading = rotated(positions, positions, frequency_ref[...])
        lane = lanes_of((TOK, 128))
        for head in range(HEADS_HERE):
            at = base + head * TOK
            query_ref[at : at + TOK, :LATENT] = jnp.dot(
                nope[:, head * NOPE : (head + 1) * NOPE],
                key_up_ref[head],
                preferred_element_type=jnp.float32,
            ).astype(jnp.bfloat16)
        for pair in range(HEADS_HERE // 2):
            turned = apply_rotation(
                rope[:, pair * 128 : (pair + 1) * 128].astype(jnp.float32),
                cosine,
                sine_value,
                leading,
            )
            for side in range(2):
                at = base + (pair * 2 + side) * TOK
                shifted = turned if side == 0 else pltpu.roll(turned, ROPE, 1)
                query_ref[at : at + TOK, LATENT:] = jnp.where(lane < ROPE, shifted, 0.0).astype(
                    jnp.bfloat16
                )

    def finish(start, product, top, total):
        acc_ref[start : start + CHUNK, :] = product
        top_ref[start : start + CHUNK, :] = jnp.broadcast_to(top, (CHUNK, 128))
        sum_ref[start : start + CHUNK, :] = total

    attend(span_ref, query_ref, [keys_ref], None, finish)


def middle_kernel(
    span_ref,
    query_ref,
    keys_ref,
    old_acc_ref,
    old_top_ref,
    old_sum_ref,
    acc_ref,
    top_ref,
    sum_ref,
):
    def finish(start, product, top, total):
        acc_ref[start : start + CHUNK, :] = product
        top_ref[start : start + CHUNK, :] = jnp.broadcast_to(top, (CHUNK, 128))
        sum_ref[start : start + CHUNK, :] = total

    attend(
        span_ref,
        query_ref,
        [keys_ref],
        (old_acc_ref, old_top_ref, old_sum_ref),
        finish,
    )


def last_kernel(
    side,
    span_ref,
    query_ref,
    one_ref,
    two_ref,
    old_acc_ref,
    old_top_ref,
    old_sum_ref,
    out_ref,
):
    def finish(start, product, top, total):
        at = start % ROWS
        whole = jnp.sum(total, axis=1, keepdims=True)
        lane = lanes_of((CHUNK, 128))
        out_ref[at : at + CHUNK, :LATENT] = product
        out_ref[at : at + CHUNK, LATENT:] = jnp.where(lane < 64, top, whole)

    attend(
        span_ref,
        query_ref,
        [one_ref, two_ref],
        (old_acc_ref, old_top_ref, old_sum_ref),
        finish,
        (side * ROWS, (side + 1) * ROWS),
    )


def merge_kernel(own_ref, got_ref, value_up_ref, out_ref):
    for head in range(HEADS_HERE):
        at = slice(head * TOK, (head + 1) * TOK)
        one_top = own_ref[at, LATENT : LATENT + 1]
        two_top = got_ref[at, LATENT : LATENT + 1]
        one_sum = own_ref[at, LATENT + 64 : LATENT + 65]
        two_sum = got_ref[at, LATENT + 64 : LATENT + 65]
        top = jnp.maximum(one_top, two_top)
        one = jnp.exp2(one_top - top)
        two = jnp.exp2(two_top - top)
        total = one_sum * one + two_sum * two
        latent = (own_ref[at, :LATENT] * one + got_ref[at, :LATENT] * two) / total
        out_ref[:, head * VDIM : (head + 1) * VDIM] = jnp.dot(
            latent.astype(jnp.bfloat16), value_up_ref[head], preferred_element_type=jnp.float32
        ).astype(jnp.bfloat16)


def call(kernel, specs, out_shape, name, vmem=32, scratch=()):
    out_specs = jax.tree.map(lambda _: VMEM, out_shape)
    return pl.pallas_call(
        kernel,
        in_specs=specs,
        out_specs=out_specs,
        out_shape=out_shape,
        name=name,
        scratch_shapes=list(scratch),
        compiler_params=pltpu.CompilerParams(vmem_limit_bytes=vmem * 1024 * 1024),
    )


def device_at(y, z, x, c):
    y, z, x = y % NY, z % (NZH * NZL), x % NX
    return (((y * NZH + z // NZL) * NC + c) * NZL + z % NZL) * NX + x


def pairs(target):
    return [
        (device_at(y, z, x, c), device_at(*target(y, z, x, c)))
        for y in range(NY)
        for z in range(NZH * NZL)
        for x in range(NX)
        for c in range(NC)
    ]


def shards(query_nope, query_rope, compressed, latent_gain, key_up, value_up, span_order):
    f32 = jnp.float32
    bf16 = jnp.bfloat16
    shape = jax.ShapeDtypeStruct
    frequency = jnp.asarray(FREQUENCY)
    def along_x(y, z, x, c):
        away = c ^ (y % 2)
        return (y, z, x + 1, 1) if away else (y, z, x - 1, 0)

    first_pairs = pairs(along_x)
    onward_pairs = pairs(lambda y, z, x, c: (y, z, x - 1 + 2 * c, c))
    relay_pairs = pairs(lambda y, z, x, c: (y - 1 + 2 * c, z, x, c))
    sibling_pairs = pairs(lambda y, z, x, c: (y, z, x, 1 - c))

    sent = call(
        prep_kernel,
        [HBM] * 4,
        shape((64, 8, WIDE), bf16),
        "prep",
        60,
        [
            pltpu.SMEM((128,), jnp.int32),
            pltpu.VMEM((8, LATENT + ROPE), bf16),
            pltpu.VMEM((1, LATENT), f32),
            pltpu.VMEM((1, 128), f32),
            pltpu.SemaphoreType.DMA((4,)),
        ],
    )(span_order, compressed, latent_gain[None], frequency)
    own_keys = lax.all_to_all(sent, PLANE, 0, 0, tiled=True).reshape(512, WIDE)
    one = lax.ppermute(own_keys, AXES, first_pairs)
    sibling = lax.ppermute(
        jnp.concatenate([query_nope, query_rope], axis=1), AXES, sibling_pairs
    )
    state = (
        shape((2 * ROWS, LATENT), f32),
        shape((2 * ROWS, 128), f32),
        shape((2 * ROWS, 128), f32),
    )
    queries, *carry = call(
        first_kernel,
        [SMEM] + [VMEM] * 6,
        (shape((2 * ROWS, WIDE), bf16), *state),
        "first",
    )(span_order, frequency, query_nope, query_rope, sibling, key_up, own_keys)
    one, carry = lax.optimization_barrier((one, carry))
    two = lax.ppermute(one, AXES, onward_pairs)
    three = lax.ppermute(one, AXES, relay_pairs)
    carry = call(middle_kernel, [SMEM] + [VMEM] * 5, state, "middle")(
        span_order, queries, one, *carry
    )
    packet = shape((ROWS, WIDE), f32)
    ending = (span_order, queries, two, three, *carry)
    send = call(functools.partial(last_kernel, 1), [SMEM] + [VMEM] * 6, packet, "last_sibling")(
        *ending
    )
    got = lax.ppermute(send, AXES, sibling_pairs)
    own = call(functools.partial(last_kernel, 0), [SMEM] + [VMEM] * 6, packet, "last_own")(*ending)
    return call(
        merge_kernel, [VMEM] * 3, shape((TOK, HEADS_HERE * VDIM), bf16), "merge", 16
    )(own, got, value_up)


def solution(mesh):
    split = Mesh(mesh.devices.reshape(NY, NZH, NC, NZL, NX), AXES)
    placed = (
        P(BLK, HEAD),
        P(BLK, HEAD),
        P(AXES, None),
        P(),
        P(HEAD, None, None),
        P(HEAD, None, None),
        P(),
    )
    return jax.shard_map(
        shards, mesh=split, in_specs=placed, out_specs=P(BLK, HEAD), check_vma=False
    )
```

```python
import functools

import jax
import jax.numpy as jnp
import numpy as np
from jax import lax
from jax.experimental import pallas as pl
from jax.experimental.pallas import tpu as pltpu
from jax.sharding import Mesh
from jax.sharding import PartitionSpec as P

AXES = ("y", "zh", "c", "zl", "x")
BLK = ("y", "zh", "c")
HEAD = ("zl", "x")
PLANE = ("y", "zh", "zl")
NY, NZH, NC, NZL, NX = 8, 4, 2, 2, 4

LATENT = 512
ROPE = 64
NOPE = 128
VDIM = 128
HEADS_HERE = 8
TOK = 64
HALF = 32
WIDE = 640
ROWS = TOK * HEADS_HERE
CHUNK = 512

norm_epsilon = 1e-06
rope_base = 10000.0
masked_score = -1e30
score_scale = (NOPE + ROPE) ** (-0.5)
log2e = 1.4426950408889634

FREQUENCY = np.tile(
    np.float32(rope_base) ** (-np.arange(ROPE // 2, dtype=np.float32) / np.float32(ROPE // 2)),
    128 // (ROPE // 2),
).astype(np.float32)[None]

VMEM = pl.BlockSpec(memory_space=pltpu.VMEM)
SMEM = pl.BlockSpec(memory_space=pltpu.SMEM)
HBM = pl.BlockSpec(memory_space=pltpu.HBM)


def lanes_of(shape):
    return lax.broadcasted_iota(jnp.int32, shape, 1)


def rotated(values, positions, frequency):
    lane = lanes_of(values.shape)
    leading = lane % ROPE < ROPE // 2
    angles = positions * frequency
    cosine = jnp.cos(angles)
    sine_value = jnp.where(leading, -jnp.sin(angles), jnp.sin(angles))
    return cosine, sine_value, leading


def apply_rotation(values, cosine, sine_value, leading):
    swapped = jnp.where(
        leading,
        pltpu.roll(values, 128 - ROPE // 2, 1),
        pltpu.roll(values, ROPE // 2, 1),
    )
    return values * cosine + swapped * sine_value


def block_index():
    return (lax.axis_index("y") * NZH + lax.axis_index("zh")) * NC + lax.axis_index("c")


def prep_kernel(
    span_hbm,
    compressed_hbm,
    gain_hbm,
    frequency_hbm,
    out_ref,
    span_ref,
    compressed_ref,
    gain_ref,
    frequency_ref,
    sems,
):
    copies = [
        pltpu.make_async_copy(source, target, sems.at[k])
        for k, (source, target) in enumerate(
            (
                (compressed_hbm, compressed_ref),
                (gain_hbm, gain_ref),
                (span_hbm, span_ref),
                (frequency_hbm, frequency_ref),
            )
        )
    ]
    for copy in copies:
        copy.start()
    for copy in copies:
        copy.wait()
    rows = compressed_ref.shape[0]
    block = block_index()
    x = lax.axis_index("x")
    span = span_ref[block * 2 + lax.axis_index("zl")]
    offset = x * rows + lax.broadcasted_iota(jnp.int32, (rows, 128), 0)
    latent = compressed_ref[:, :LATENT].astype(jnp.float32)
    scale = lax.rsqrt(jnp.mean(latent * latent, axis=1, keepdims=True) + norm_epsilon)
    latent = (latent * scale * gain_ref[...]).astype(jnp.bfloat16)
    rope = compressed_ref[:, LATENT:].astype(jnp.float32)
    rope = jnp.concatenate([rope, jnp.zeros_like(rope)], axis=1)
    positions = (span * HALF + offset).astype(jnp.float32)
    cosine, sine_value, leading = rotated(rope, positions, frequency_ref[...])
    turned = apply_rotation(rope, cosine, sine_value, leading)
    lane = lanes_of((rows, 128))
    tail = jnp.where(
        lane < ROPE,
        turned,
        jnp.where(
            lane == ROPE,
            span.astype(jnp.float32),
            jnp.where(lane == ROPE + 1, offset.astype(jnp.float32), 0.0),
        ),
    ).astype(jnp.bfloat16)
    row = jnp.concatenate([latent, tail], axis=1)
    out_ref[...] = jnp.broadcast_to(row[None], out_ref.shape)


def key_positions(keys):
    lane = lanes_of((16, WIDE))
    pick = jnp.where(
        lane == LATENT + ROPE, float(HALF), jnp.where(lane == LATENT + ROPE + 1, 1.0, 0.0)
    ).astype(jnp.bfloat16)
    found = lax.dot_general(
        pick, keys, (((1,), (1,)), ((), ())), preferred_element_type=jnp.float32
    )
    return found[:8]


def query_positions(span_ref, other):
    block = block_index() + other * (1 - 2 * lax.axis_index("c"))
    token = lax.broadcasted_iota(jnp.int32, (TOK, 128), 0)
    first = span_ref[block * 2] * HALF
    second = span_ref[block * 2 + 1] * HALF - HALF
    return (token + jnp.where(token < HALF, first, second)).astype(jnp.float32)


def attend(query_ref, place_ref, key_refs, carry, finish, rows=(0, 2 * ROWS)):
    keys = [ref[...] for ref in key_refs]
    places = [key_positions(block) for block in keys]
    for start in range(*rows, CHUNK):
        queries = query_ref[start : start + CHUNK, :]
        here = place_ref[start : start + CHUNK, :]
        scores = []
        for block, place in zip(keys, places):
            raw = lax.dot_general(
                queries, block, (((1,), (1,)), ((), ())), preferred_element_type=jnp.float32
            )
            pieces = []
            for at in range(0, block.shape[0], 128):
                there = jnp.tile(place[:, at : at + 128], (CHUNK // 8, 1))
                pieces.append(
                    jnp.where(
                        there <= here, raw[:, at : at + 128] * (score_scale * log2e), masked_score
                    )
                )
            scores.append(pieces)
        top = functools.reduce(jnp.maximum, [piece for pieces in scores for piece in pieces])
        top = jnp.broadcast_to(jnp.max(top, axis=1, keepdims=True), (CHUNK, 128))
        if carry is not None:
            old_acc, old_top, old_sum = carry
            before = old_top[start : start + CHUNK, :]
            top = jnp.maximum(top, before)
        product = None
        total = None
        for block, pieces in zip(keys, scores):
            weights = [jnp.exp2(piece - top) for piece in pieces]
            for weight in weights:
                total = weight if total is None else total + weight
            term = jnp.dot(
                jnp.concatenate([weight.astype(jnp.bfloat16) for weight in weights], axis=1),
                block[:, :LATENT],
                preferred_element_type=jnp.float32,
            )
            product = term if product is None else product + term
        if carry is not None:
            shrink = jnp.exp2(before - top)
            product = product + old_acc[start : start + CHUNK, :] * jnp.tile(
                shrink, (1, LATENT // 128)
            )
            total = total + old_sum[start : start + CHUNK, :] * shrink
        finish(start, product, top, total)


def keep(acc_ref, top_ref, sum_ref):
    def finish(start, product, top, total):
        acc_ref[start : start + CHUNK, :] = product
        top_ref[start : start + CHUNK, :] = top
        sum_ref[start : start + CHUNK, :] = total

    return finish


def first_kernel(
    span_ref,
    frequency_ref,
    nope_ref,
    rope_ref,
    sibling_ref,
    key_up_ref,
    keys_ref,
    query_ref,
    place_ref,
    acc_ref,
    top_ref,
    sum_ref,
):
    nope = jnp.concatenate([nope_ref[...], sibling_ref[:, : HEADS_HERE * NOPE]], axis=0)
    rope = jnp.concatenate([rope_ref[...], sibling_ref[:, HEADS_HERE * NOPE :]], axis=0)
    positions = jnp.concatenate([query_positions(span_ref, other) for other in range(2)], axis=0)
    cosine, sine_value, leading = rotated(positions, positions, frequency_ref[...])
    lane = lanes_of((2 * TOK, 128))
    for head in range(HEADS_HERE):
        raised = jnp.dot(
            nope[:, head * NOPE : (head + 1) * NOPE],
            key_up_ref[head],
            preferred_element_type=jnp.float32,
        ).astype(jnp.bfloat16)
        if head % 2 == 0:
            turned = apply_rotation(
                rope[:, head * ROPE : head * ROPE + 128].astype(jnp.float32),
                cosine,
                sine_value,
                leading,
            )
        else:
            turned = pltpu.roll(turned, ROPE, 1)
        tail = jnp.where(lane < ROPE, turned, 0.0).astype(jnp.bfloat16)
        for other in range(2):
            at = other * ROWS + head * TOK
            query_ref[at : at + TOK, :LATENT] = raised[other * TOK : (other + 1) * TOK]
            query_ref[at : at + TOK, LATENT:] = tail[other * TOK : (other + 1) * TOK]
            place_ref[at : at + TOK, :] = positions[other * TOK : (other + 1) * TOK]
    attend(query_ref, place_ref, [keys_ref], None, keep(acc_ref, top_ref, sum_ref))


def middle_kernel(count, query_ref, place_ref, *refs):
    old = refs[count : count + 3]
    attend(query_ref, place_ref, refs[:count], old, keep(*refs[count + 3 :]))


def last_kernel(
    side, query_ref, place_ref, keys_ref, old_acc_ref, old_top_ref, old_sum_ref, out_ref
):
    def finish(start, product, top, total):
        at = start % ROWS
        whole = jnp.sum(total, axis=1, keepdims=True)
        lane = lanes_of((CHUNK, 128))
        out_ref[at : at + CHUNK, :LATENT] = product
        out_ref[at : at + CHUNK, LATENT:] = jnp.where(lane < 64, top, whole)

    attend(
        query_ref,
        place_ref,
        [keys_ref],
        (old_acc_ref, old_top_ref, old_sum_ref),
        finish,
        (side * ROWS, (side + 1) * ROWS),
    )


def merge_kernel(own_ref, got_ref, value_up_ref, out_ref):
    for head in range(HEADS_HERE):
        at = slice(head * TOK, (head + 1) * TOK)
        one_top = own_ref[at, LATENT : LATENT + 1]
        two_top = got_ref[at, LATENT : LATENT + 1]
        one_sum = own_ref[at, LATENT + 64 : LATENT + 65]
        two_sum = got_ref[at, LATENT + 64 : LATENT + 65]
        top = jnp.maximum(one_top, two_top)
        one = jnp.exp2(one_top - top)
        two = jnp.exp2(two_top - top)
        total = one_sum * one + two_sum * two
        latent = (own_ref[at, :LATENT] * one + got_ref[at, :LATENT] * two) / total
        out_ref[:, head * VDIM : (head + 1) * VDIM] = jnp.dot(
            latent.astype(jnp.bfloat16), value_up_ref[head], preferred_element_type=jnp.float32
        ).astype(jnp.bfloat16)


def call(kernel, specs, out_shape, name, vmem=32, scratch=()):
    out_specs = jax.tree.map(lambda _: VMEM, out_shape)
    return pl.pallas_call(
        kernel,
        in_specs=specs,
        out_specs=out_specs,
        out_shape=out_shape,
        name=name,
        scratch_shapes=list(scratch),
        compiler_params=pltpu.CompilerParams(vmem_limit_bytes=vmem * 1024 * 1024),
    )


def device_at(y, z, x, c):
    y, z, x = y % NY, z % (NZH * NZL), x % NX
    return (((y * NZH + z // NZL) * NC + c) * NZL + z % NZL) * NX + x


def pairs(target):
    return [
        (device_at(y, z, x, c), device_at(*target(y, z, x, c)))
        for y in range(NY)
        for z in range(NZH * NZL)
        for x in range(NX)
        for c in range(NC)
    ]


def shards(query_nope, query_rope, compressed, latent_gain, key_up, value_up, span_order):
    f32 = jnp.float32
    bf16 = jnp.bfloat16
    shape = jax.ShapeDtypeStruct
    frequency = jnp.asarray(FREQUENCY)
    def along_x(y, z, x, c):
        away = c ^ ((y + z) % 2)
        return (y, z, x + 1, 1) if away else (y, z, x - 1, 0)

    first_pairs = pairs(along_x)
    onward_pairs = pairs(lambda y, z, x, c: (y, z, x - 1 + 2 * c, c))
    y_pairs = pairs(lambda y, z, x, c: (y - 1 + 2 * c, z, x, c))
    z_pairs = pairs(lambda y, z, x, c: (y, z - 1 + 2 * c, x, c))
    sibling_pairs = pairs(lambda y, z, x, c: (y, z, x, 1 - c))

    sent = call(
        prep_kernel,
        [HBM] * 4,
        shape((64, 8, WIDE), bf16),
        "prep",
        60,
        [
            pltpu.SMEM((128,), jnp.int32),
            pltpu.VMEM((8, LATENT + ROPE), bf16),
            pltpu.VMEM((1, LATENT), f32),
            pltpu.VMEM((1, 128), f32),
            pltpu.SemaphoreType.DMA((4,)),
        ],
    )(span_order, compressed, latent_gain[None], frequency)
    own_keys = lax.all_to_all(sent, PLANE, 0, 0, tiled=True).reshape(512, WIDE)
    one = lax.ppermute(own_keys, AXES, first_pairs)
    sibling = lax.ppermute(
        jnp.concatenate([query_nope, query_rope], axis=1), AXES, sibling_pairs
    )
    state = (
        shape((2 * ROWS, LATENT), f32),
        shape((2 * ROWS, 128), f32),
        shape((2 * ROWS, 128), f32),
    )
    queries, places, *carry = call(
        first_kernel,
        [SMEM] + [VMEM] * 6,
        (shape((2 * ROWS, WIDE), bf16), shape((2 * ROWS, 128), f32), *state),
        "first",
    )(span_order, frequency, query_nope, query_rope, sibling, key_up, own_keys)
    one, carry = lax.optimization_barrier((one, carry))
    four = lax.ppermute(one, AXES, onward_pairs)
    two = lax.ppermute(one[:256], AXES, y_pairs)
    three = lax.ppermute(one[256:], AXES, z_pairs)
    carry = call(functools.partial(middle_kernel, 1), [VMEM] * 6, state, "middle_x")(
        queries, places, one, *carry
    )
    carry = call(functools.partial(middle_kernel, 2), [VMEM] * 7, state, "middle_yz")(
        queries, places, two, three, *carry
    )
    packet = shape((ROWS, WIDE), f32)
    ending = (queries, places, four, *carry)
    send = call(functools.partial(last_kernel, 1), [VMEM] * 6, packet, "last_sibling")(*ending)
    got = lax.ppermute(send, AXES, sibling_pairs)
    own = call(functools.partial(last_kernel, 0), [VMEM] * 6, packet, "last_own")(*ending)
    return call(
        merge_kernel, [VMEM] * 3, shape((TOK, HEADS_HERE * VDIM), bf16), "merge", 16
    )(own, got, value_up)


def solution(mesh):
    split = Mesh(mesh.devices.reshape(NY, NZH, NC, NZL, NX), AXES)
    placed = (
        P(BLK, HEAD),
        P(BLK, HEAD),
        P(AXES, None),
        P(),
        P(HEAD, None, None),
        P(HEAD, None, None),
        P(),
    )
    return jax.shard_map(
        shards, mesh=split, in_specs=placed, out_specs=P(BLK, HEAD), check_vma=False
    )
```

```python
import functools

import jax
import jax.numpy as jnp
import numpy as np
from jax import lax
from jax.experimental import pallas as pl
from jax.experimental.pallas import tpu as pltpu
from jax.sharding import Mesh
from jax.sharding import PartitionSpec as P

AXES = ("y", "zh", "c", "zl", "x")
BLK = ("y", "zh", "c")
HEAD = ("zl", "x")
PLANE = ("y", "zh", "zl")
NY, NZH, NC, NZL, NX = 8, 4, 2, 2, 4

LATENT = 512
ROPE = 64
NOPE = 128
VDIM = 128
HEADS_HERE = 8
TOK = 64
HALF = 32
WIDE = 640
ROWS = TOK * HEADS_HERE
CHUNK = 512

norm_epsilon = 1e-06
rope_base = 10000.0
masked_score = -1e30
score_scale = (NOPE + ROPE) ** (-0.5)
log2e = 1.4426950408889634

FREQUENCY = np.tile(
    np.float32(rope_base) ** (-np.arange(ROPE // 2, dtype=np.float32) / np.float32(ROPE // 2)),
    128 // (ROPE // 2),
).astype(np.float32)[None]

VMEM = pl.BlockSpec(memory_space=pltpu.VMEM)
SMEM = pl.BlockSpec(memory_space=pltpu.SMEM)
HBM = pl.BlockSpec(memory_space=pltpu.HBM)


def lanes_of(shape):
    return lax.broadcasted_iota(jnp.int32, shape, 1)


def rotated(values, positions, frequency):
    lane = lanes_of(values.shape)
    leading = lane % ROPE < ROPE // 2
    angles = positions * frequency
    cosine = jnp.cos(angles)
    sine_value = jnp.where(leading, -jnp.sin(angles), jnp.sin(angles))
    return cosine, sine_value, leading


def apply_rotation(values, cosine, sine_value, leading):
    swapped = jnp.where(
        leading,
        pltpu.roll(values, 128 - ROPE // 2, 1),
        pltpu.roll(values, ROPE // 2, 1),
    )
    return values * cosine + swapped * sine_value


def block_index():
    return (lax.axis_index("y") * NZH + lax.axis_index("zh")) * NC + lax.axis_index("c")


def prep_kernel(
    span_hbm,
    compressed_hbm,
    gain_hbm,
    frequency_hbm,
    out_ref,
    span_ref,
    compressed_ref,
    gain_ref,
    frequency_ref,
    sems,
):
    copies = [
        pltpu.make_async_copy(source, target, sems.at[k])
        for k, (source, target) in enumerate(
            (
                (compressed_hbm, compressed_ref),
                (gain_hbm, gain_ref),
                (span_hbm, span_ref),
                (frequency_hbm, frequency_ref),
            )
        )
    ]
    for copy in copies:
        copy.start()
    for copy in copies:
        copy.wait()
    rows = compressed_ref.shape[0]
    block = block_index()
    x = lax.axis_index("x")
    span = span_ref[block * 2 + lax.axis_index("zl")]
    offset = x * rows + lax.broadcasted_iota(jnp.int32, (rows, 128), 0)
    latent = compressed_ref[:, :LATENT].astype(jnp.float32)
    scale = lax.rsqrt(jnp.mean(latent * latent, axis=1, keepdims=True) + norm_epsilon)
    latent = (latent * scale * gain_ref[...]).astype(jnp.bfloat16)
    rope = compressed_ref[:, LATENT:].astype(jnp.float32)
    rope = jnp.concatenate([rope, jnp.zeros_like(rope)], axis=1)
    positions = (span * HALF + offset).astype(jnp.float32)
    cosine, sine_value, leading = rotated(rope, positions, frequency_ref[...])
    turned = apply_rotation(rope, cosine, sine_value, leading)
    lane = lanes_of((rows, 128))
    tail = jnp.where(
        lane < ROPE,
        turned,
        jnp.where(
            lane == ROPE,
            span.astype(jnp.float32),
            jnp.where(lane == ROPE + 1, offset.astype(jnp.float32), 0.0),
        ),
    ).astype(jnp.bfloat16)
    row = jnp.concatenate([latent, tail], axis=1)
    out_ref[...] = jnp.broadcast_to(row[None], out_ref.shape)


def key_positions(keys):
    lane = lanes_of((16, WIDE))
    pick = jnp.where(
        lane == LATENT + ROPE, float(HALF), jnp.where(lane == LATENT + ROPE + 1, 1.0, 0.0)
    ).astype(jnp.bfloat16)
    found = lax.dot_general(
        pick, keys, (((1,), (1,)), ((), ())), preferred_element_type=jnp.float32
    )
    return found[:8]


def query_positions(span_ref, other):
    block = block_index() + other * (1 - 2 * lax.axis_index("c"))
    token = lax.broadcasted_iota(jnp.int32, (TOK, 128), 0)
    first = span_ref[block * 2] * HALF
    second = span_ref[block * 2 + 1] * HALF - HALF
    return (token + jnp.where(token < HALF, first, second)).astype(jnp.float32)


def attend(query_ref, place_ref, key_refs, carry, finish, rows=(0, 2 * ROWS)):
    keys = [ref[...] for ref in key_refs]
    places = [key_positions(block) for block in keys]
    for start in range(*rows, CHUNK):
        queries = query_ref[start : start + CHUNK, :]
        here = place_ref[start : start + CHUNK, :]
        scores = []
        for block, place in zip(keys, places):
            raw = lax.dot_general(
                queries, block, (((1,), (1,)), ((), ())), preferred_element_type=jnp.float32
            )
            pieces = []
            for at in range(0, block.shape[0], 128):
                there = jnp.tile(place[:, at : at + 128], (CHUNK // 8, 1))
                pieces.append(
                    jnp.where(
                        there <= here, raw[:, at : at + 128] * (score_scale * log2e), masked_score
                    )
                )
            scores.append(pieces)
        top = functools.reduce(jnp.maximum, [piece for pieces in scores for piece in pieces])
        top = jnp.broadcast_to(jnp.max(top, axis=1, keepdims=True), (CHUNK, 128))
        if carry is not None:
            old_acc, old_top, old_sum = carry
            before = old_top[start : start + CHUNK, :]
            top = jnp.maximum(top, before)
        product = None
        total = None
        for block, pieces in zip(keys, scores):
            weights = [jnp.exp2(piece - top) for piece in pieces]
            for weight in weights:
                total = weight if total is None else total + weight
            term = jnp.dot(
                jnp.concatenate([weight.astype(jnp.bfloat16) for weight in weights], axis=1),
                block[:, :LATENT],
                preferred_element_type=jnp.float32,
            )
            product = term if product is None else product + term
        if carry is not None:
            shrink = jnp.exp2(before - top)
            product = product + old_acc[start : start + CHUNK, :] * jnp.tile(
                shrink, (1, LATENT // 128)
            )
            total = total + old_sum[start : start + CHUNK, :] * shrink
        finish(start, product, top, total)


def keep(acc_ref, top_ref, sum_ref):
    def finish(start, product, top, total):
        acc_ref[start : start + CHUNK, :] = product
        top_ref[start : start + CHUNK, :] = top
        sum_ref[start : start + CHUNK, :] = total

    return finish


def first_kernel(
    span_ref,
    frequency_ref,
    nope_ref,
    rope_ref,
    sibling_ref,
    key_up_ref,
    keys_ref,
    query_ref,
    place_ref,
    acc_ref,
    top_ref,
    sum_ref,
):
    nope = jnp.concatenate([nope_ref[...], sibling_ref[:, : HEADS_HERE * NOPE]], axis=0)
    rope = jnp.concatenate([rope_ref[...], sibling_ref[:, HEADS_HERE * NOPE :]], axis=0)
    positions = jnp.concatenate([query_positions(span_ref, other) for other in range(2)], axis=0)
    cosine, sine_value, leading = rotated(positions, positions, frequency_ref[...])
    lane = lanes_of((2 * TOK, 128))
    for head in range(HEADS_HERE):
        raised = jnp.dot(
            nope[:, head * NOPE : (head + 1) * NOPE],
            key_up_ref[head],
            preferred_element_type=jnp.float32,
        ).astype(jnp.bfloat16)
        if head % 2 == 0:
            turned = apply_rotation(
                rope[:, head * ROPE : head * ROPE + 128].astype(jnp.float32),
                cosine,
                sine_value,
                leading,
            )
        else:
            turned = pltpu.roll(turned, ROPE, 1)
        tail = jnp.where(lane < ROPE, turned, 0.0).astype(jnp.bfloat16)
        for other in range(2):
            at = other * ROWS + head * TOK
            query_ref[at : at + TOK, :LATENT] = raised[other * TOK : (other + 1) * TOK]
            query_ref[at : at + TOK, LATENT:] = tail[other * TOK : (other + 1) * TOK]
            place_ref[at : at + TOK, :] = positions[other * TOK : (other + 1) * TOK]
    attend(query_ref, place_ref, [keys_ref], None, keep(acc_ref, top_ref, sum_ref))


def middle_kernel(
    query_ref,
    place_ref,
    keys_ref,
    old_acc_ref,
    old_top_ref,
    old_sum_ref,
    acc_ref,
    top_ref,
    sum_ref,
):
    old = (old_acc_ref, old_top_ref, old_sum_ref)
    attend(query_ref, place_ref, [keys_ref], old, keep(acc_ref, top_ref, sum_ref))


def send_kernel(query_ref, place_ref, keys_ref, old_acc_ref, old_top_ref, old_sum_ref, out_ref):
    def finish(start, product, top, total):
        at = start % ROWS
        whole = jnp.broadcast_to(jnp.sum(total, axis=1, keepdims=True), (CHUNK, 128))
        lane = lanes_of((CHUNK, 128))
        level = top + jnp.log2(whole)
        high = level.astype(jnp.bfloat16).astype(jnp.float32)
        rest = level - high
        middle = rest.astype(jnp.bfloat16).astype(jnp.float32)
        low = rest - middle
        pieces = jnp.where(
            lane == 0, high, jnp.where(lane == 1, middle, jnp.where(lane == 2, low, 0.0))
        )
        inverse = jnp.tile(1.0 / whole, (1, LATENT // 128))
        out_ref[at : at + CHUNK, :LATENT] = (product * inverse).astype(jnp.bfloat16)
        out_ref[at : at + CHUNK, LATENT:] = pieces.astype(jnp.bfloat16)

    old = (old_acc_ref, old_top_ref, old_sum_ref)
    attend(query_ref, place_ref, [keys_ref], old, finish, (ROWS, 2 * ROWS))


def own_kernel(
    query_ref,
    place_ref,
    keys_ref,
    old_acc_ref,
    old_top_ref,
    old_sum_ref,
    acc_ref,
    top_ref,
    sum_ref,
):
    def finish(start, product, top, total):
        acc_ref[start : start + CHUNK, :] = product
        top_ref[start : start + CHUNK, :] = top
        sum_ref[start : start + CHUNK, :] = jnp.broadcast_to(
            jnp.sum(total, axis=1, keepdims=True), (CHUNK, 128)
        )

    old = (old_acc_ref, old_top_ref, old_sum_ref)
    attend(query_ref, place_ref, [keys_ref], old, finish, (0, ROWS))


def merge_kernel(acc_ref, top_ref, sum_ref, got_ref, value_up_ref, out_ref):
    for head in range(HEADS_HERE):
        at = slice(head * TOK, (head + 1) * TOK)
        level = jnp.sum(got_ref[at, LATENT:].astype(jnp.float32), axis=1, keepdims=True)
        level = jnp.broadcast_to(level, (TOK, 128))
        own_top = top_ref[at, :]
        top = jnp.maximum(own_top, level)
        one = jnp.exp2(own_top - top)
        two = jnp.exp2(level - top)
        inverse = 1.0 / (sum_ref[at, :] * one + two)
        one = jnp.tile(one * inverse, (1, LATENT // 128))
        two = jnp.tile(two * inverse, (1, LATENT // 128))
        latent = acc_ref[at, :] * one + got_ref[at, :LATENT].astype(jnp.float32) * two
        out_ref[:, head * VDIM : (head + 1) * VDIM] = jnp.dot(
            latent.astype(jnp.bfloat16), value_up_ref[head], preferred_element_type=jnp.float32
        ).astype(jnp.bfloat16)


def call(kernel, specs, out_shape, name, vmem=32, scratch=()):
    out_specs = jax.tree.map(lambda _: VMEM, out_shape)
    return pl.pallas_call(
        kernel,
        in_specs=specs,
        out_specs=out_specs,
        out_shape=out_shape,
        name=name,
        scratch_shapes=list(scratch),
        compiler_params=pltpu.CompilerParams(vmem_limit_bytes=vmem * 1024 * 1024),
    )


def device_at(y, z, x, c):
    y, z, x = y % NY, z % (NZH * NZL), x % NX
    return (((y * NZH + z // NZL) * NC + c) * NZL + z % NZL) * NX + x


def pairs(target):
    return [
        (device_at(y, z, x, c), device_at(*target(y, z, x, c)))
        for y in range(NY)
        for z in range(NZH * NZL)
        for x in range(NX)
        for c in range(NC)
    ]


def shards(query_nope, query_rope, compressed, latent_gain, key_up, value_up, span_order):
    f32 = jnp.float32
    bf16 = jnp.bfloat16
    shape = jax.ShapeDtypeStruct
    frequency = jnp.asarray(FREQUENCY)
    def along_x(y, z, x, c):
        away = c ^ (y % 2)
        return (y, z, x + 1, 1) if away else (y, z, x - 1, 0)

    first_pairs = pairs(along_x)
    onward_pairs = pairs(lambda y, z, x, c: (y, z, x - 1 + 2 * c, c))
    y_pairs = pairs(lambda y, z, x, c: (y - 1 + 2 * c, z, x, c))
    sibling_pairs = pairs(lambda y, z, x, c: (y, z, x, 1 - c))

    sent = call(
        prep_kernel,
        [HBM] * 4,
        shape((64, 8, WIDE), bf16),
        "prep",
        60,
        [
            pltpu.SMEM((128,), jnp.int32),
            pltpu.VMEM((8, LATENT + ROPE), bf16),
            pltpu.VMEM((1, LATENT), f32),
            pltpu.VMEM((1, 128), f32),
            pltpu.SemaphoreType.DMA((4,)),
        ],
    )(span_order, compressed, latent_gain[None], frequency)
    own_keys = lax.all_to_all(sent, PLANE, 0, 0, tiled=True).reshape(512, WIDE)
    one = lax.ppermute(own_keys, AXES, first_pairs)
    sibling = lax.ppermute(
        jnp.concatenate([query_nope, query_rope], axis=1), AXES, sibling_pairs
    )
    state = (
        shape((2 * ROWS, LATENT), f32),
        shape((2 * ROWS, 128), f32),
        shape((2 * ROWS, 128), f32),
    )
    queries, places, *carry = call(
        first_kernel,
        [SMEM] + [VMEM] * 6,
        (shape((2 * ROWS, WIDE), bf16), shape((2 * ROWS, 128), f32), *state),
        "first",
    )(span_order, frequency, query_nope, query_rope, sibling, key_up, own_keys)
    one, carry = lax.optimization_barrier((one, carry))
    two = lax.ppermute(one, AXES, onward_pairs)
    three = lax.ppermute(one, AXES, y_pairs)
    middle = call(middle_kernel, [VMEM] * 6, state, "middle")
    carry = middle(queries, places, one, *carry)
    carry = middle(queries, places, two, *carry)
    ending = (queries, places, three, *carry)
    send = call(send_kernel, [VMEM] * 6, shape((ROWS, WIDE), bf16), "sibling_rows")(*ending)
    got = lax.ppermute(send, AXES, sibling_pairs)
    own_state = (
        shape((ROWS, LATENT), f32),
        shape((ROWS, 128), f32),
        shape((ROWS, 128), f32),
    )
    own = call(own_kernel, [VMEM] * 6, own_state, "own_rows")(*ending)
    return call(
        merge_kernel, [VMEM] * 5, shape((TOK, HEADS_HERE * VDIM), bf16), "merge", 16
    )(*own, got, value_up)


def solution(mesh):
    split = Mesh(mesh.devices.reshape(NY, NZH, NC, NZL, NX), AXES)
    placed = (
        P(BLK, HEAD),
        P(BLK, HEAD),
        P(AXES, None),
        P(),
        P(HEAD, None, None),
        P(HEAD, None, None),
        P(),
    )
    return jax.shard_map(
        shards, mesh=split, in_specs=placed, out_specs=P(BLK, HEAD), check_vma=False
    )
```

```python
import functools

import jax
import jax.numpy as jnp
import numpy as np
from jax import lax
from jax.experimental import pallas as pl
from jax.experimental.pallas import tpu as pltpu
from jax.sharding import Mesh
from jax.sharding import PartitionSpec as P

AXES = ("y", "zh", "c", "zl", "x")
BLK = ("y", "zh", "c")
HEAD = ("zl", "x")
NY, NZH, NC, NZL, NX = 8, 4, 2, 2, 4

LATENT = 512
ROPE = 64
NOPE = 128
VDIM = 128
HEADS_HERE = 8
TOK = 64
HALF = 32
WIDE = 640
ROWS = TOK * HEADS_HERE
CHUNK = 512

norm_epsilon = 1e-06
rope_base = 10000.0
masked_score = -1e30
score_scale = (NOPE + ROPE) ** (-0.5)
log2e = 1.4426950408889634

FREQUENCY = np.tile(
    np.float32(rope_base) ** (-np.arange(ROPE // 2, dtype=np.float32) / np.float32(ROPE // 2)),
    128 // (ROPE // 2),
).astype(np.float32)[None]

VMEM = pl.BlockSpec(memory_space=pltpu.VMEM)
SMEM = pl.BlockSpec(memory_space=pltpu.SMEM)
HBM = pl.BlockSpec(memory_space=pltpu.HBM)


def lanes_of(shape):
    return lax.broadcasted_iota(jnp.int32, shape, 1)


def rotated(values, positions, frequency):
    lane = lanes_of(values.shape)
    leading = lane % ROPE < ROPE // 2
    angles = positions * frequency
    cosine = jnp.cos(angles)
    sine_value = jnp.where(leading, -jnp.sin(angles), jnp.sin(angles))
    return cosine, sine_value, leading


def apply_rotation(values, cosine, sine_value, leading):
    swapped = jnp.where(
        leading,
        pltpu.roll(values, 128 - ROPE // 2, 1),
        pltpu.roll(values, ROPE // 2, 1),
    )
    return values * cosine + swapped * sine_value


def block_index():
    return (lax.axis_index("y") * NZH + lax.axis_index("zh")) * NC + lax.axis_index("c")


def prep_kernel(
    span_hbm,
    compressed_hbm,
    gain_hbm,
    frequency_hbm,
    out_ref,
    span_ref,
    compressed_ref,
    gain_ref,
    frequency_ref,
    sems,
):
    copies = [
        pltpu.make_async_copy(source, target, sems.at[k])
        for k, (source, target) in enumerate(
            (
                (compressed_hbm, compressed_ref),
                (gain_hbm, gain_ref),
                (span_hbm, span_ref),
                (frequency_hbm, frequency_ref),
            )
        )
    ]
    for copy in copies:
        copy.start()
    for copy in copies:
        copy.wait()
    rows = compressed_ref.shape[0]
    block = block_index()
    x = lax.axis_index("x")
    span = span_ref[block * 2 + lax.axis_index("zl")]
    offset = x * rows + lax.broadcasted_iota(jnp.int32, (rows, 128), 0)
    latent = compressed_ref[:, :LATENT].astype(jnp.float32)
    scale = lax.rsqrt(jnp.mean(latent * latent, axis=1, keepdims=True) + norm_epsilon)
    latent = (latent * scale * gain_ref[...]).astype(jnp.bfloat16)
    rope = compressed_ref[:, LATENT:].astype(jnp.float32)
    rope = jnp.concatenate([rope, jnp.zeros_like(rope)], axis=1)
    positions = (span * HALF + offset).astype(jnp.float32)
    cosine, sine_value, leading = rotated(rope, positions, frequency_ref[...])
    turned = apply_rotation(rope, cosine, sine_value, leading)
    lane = lanes_of((rows, 128))
    tail = jnp.where(
        lane < ROPE,
        turned,
        jnp.where(
            lane == ROPE,
            span.astype(jnp.float32),
            jnp.where(lane == ROPE + 1, offset.astype(jnp.float32), 0.0),
        ),
    ).astype(jnp.bfloat16)
    row = jnp.concatenate([latent, tail], axis=1)
    out_ref[...] = jnp.broadcast_to(row[None], out_ref.shape)


def key_positions(keys):
    lane = lanes_of((16, WIDE))
    pick = jnp.where(
        lane == LATENT + ROPE, float(HALF), jnp.where(lane == LATENT + ROPE + 1, 1.0, 0.0)
    ).astype(jnp.bfloat16)
    found = lax.dot_general(
        pick, keys, (((1,), (1,)), ((), ())), preferred_element_type=jnp.float32
    )
    return found[:8]


def query_positions(span_ref, other):
    block = block_index() + other * (1 - 2 * lax.axis_index("c"))
    token = lax.broadcasted_iota(jnp.int32, (TOK, 128), 0)
    first = span_ref[block * 2] * HALF
    second = span_ref[block * 2 + 1] * HALF - HALF
    return (token + jnp.where(token < HALF, first, second)).astype(jnp.float32)


def attend(query_ref, place_ref, key_refs, carry, finish, rows=(0, 2 * ROWS)):
    keys = [ref[...] for ref in key_refs]
    places = [key_positions(block) for block in keys]
    for start in range(*rows, CHUNK):
        queries = query_ref[start : start + CHUNK, :]
        here = place_ref[start : start + CHUNK, :]
        scores = []
        for block, place in zip(keys, places):
            raw = lax.dot_general(
                queries, block, (((1,), (1,)), ((), ())), preferred_element_type=jnp.float32
            )
            pieces = []
            for at in range(0, block.shape[0], 128):
                there = jnp.tile(place[:, at : at + 128], (CHUNK // 8, 1))
                pieces.append(
                    jnp.where(
                        there <= here, raw[:, at : at + 128] * (score_scale * log2e), masked_score
                    )
                )
            scores.append(pieces)
        top = functools.reduce(jnp.maximum, [piece for pieces in scores for piece in pieces])
        top = jnp.broadcast_to(jnp.max(top, axis=1, keepdims=True), (CHUNK, 128))
        if carry is not None:
            old_acc, old_top, old_sum = carry
            before = old_top[start : start + CHUNK, :]
            top = jnp.maximum(top, before)
        product = None
        total = None
        for block, pieces in zip(keys, scores):
            weights = [jnp.exp2(piece - top) for piece in pieces]
            for weight in weights:
                total = weight if total is None else total + weight
            term = jnp.dot(
                jnp.concatenate([weight.astype(jnp.bfloat16) for weight in weights], axis=1),
                block[:, :LATENT],
                preferred_element_type=jnp.float32,
            )
            product = term if product is None else product + term
        if carry is not None:
            shrink = jnp.exp2(before - top)
            product = product + old_acc[start : start + CHUNK, :] * jnp.tile(
                shrink, (1, LATENT // 128)
            )
            total = total + old_sum[start : start + CHUNK, :] * shrink
        finish(start, product, top, total)


def keep(acc_ref, top_ref, sum_ref):
    def finish(start, product, top, total):
        acc_ref[start : start + CHUNK, :] = product
        top_ref[start : start + CHUNK, :] = top
        sum_ref[start : start + CHUNK, :] = total

    return finish


def first_kernel(
    span_ref,
    frequency_ref,
    nope_ref,
    rope_ref,
    sibling_ref,
    key_up_ref,
    keys_ref,
    query_ref,
    place_ref,
    acc_ref,
    top_ref,
    sum_ref,
):
    nope = jnp.concatenate([nope_ref[...], sibling_ref[:, : HEADS_HERE * NOPE]], axis=0)
    rope = jnp.concatenate([rope_ref[...], sibling_ref[:, HEADS_HERE * NOPE :]], axis=0)
    positions = jnp.concatenate([query_positions(span_ref, other) for other in range(2)], axis=0)
    cosine, sine_value, leading = rotated(positions, positions, frequency_ref[...])
    lane = lanes_of((2 * TOK, 128))
    for head in range(HEADS_HERE):
        raised = jnp.dot(
            nope[:, head * NOPE : (head + 1) * NOPE],
            key_up_ref[head],
            preferred_element_type=jnp.float32,
        ).astype(jnp.bfloat16)
        if head % 2 == 0:
            turned = apply_rotation(
                rope[:, head * ROPE : head * ROPE + 128].astype(jnp.float32),
                cosine,
                sine_value,
                leading,
            )
        else:
            turned = pltpu.roll(turned, ROPE, 1)
        tail = jnp.where(lane < ROPE, turned, 0.0).astype(jnp.bfloat16)
        for other in range(2):
            at = other * ROWS + head * TOK
            query_ref[at : at + TOK, :LATENT] = raised[other * TOK : (other + 1) * TOK]
            query_ref[at : at + TOK, LATENT:] = tail[other * TOK : (other + 1) * TOK]
            place_ref[at : at + TOK, :] = positions[other * TOK : (other + 1) * TOK]
    attend(query_ref, place_ref, [keys_ref], None, keep(acc_ref, top_ref, sum_ref))


def middle_kernel(
    query_ref,
    place_ref,
    one_ref,
    two_ref,
    old_acc_ref,
    old_top_ref,
    old_sum_ref,
    acc_ref,
    top_ref,
    sum_ref,
):
    old = (old_acc_ref, old_top_ref, old_sum_ref)
    attend(query_ref, place_ref, [one_ref, two_ref], old, keep(acc_ref, top_ref, sum_ref))


def send_kernel(query_ref, place_ref, keys_ref, old_acc_ref, old_top_ref, old_sum_ref, out_ref):
    def finish(start, product, top, total):
        at = start % ROWS
        whole = jnp.broadcast_to(jnp.sum(total, axis=1, keepdims=True), (CHUNK, 128))
        lane = lanes_of((CHUNK, 128))
        level = top + jnp.log2(whole)
        high = level.astype(jnp.bfloat16).astype(jnp.float32)
        rest = level - high
        middle = rest.astype(jnp.bfloat16).astype(jnp.float32)
        low = rest - middle
        pieces = jnp.where(
            lane == 0, high, jnp.where(lane == 1, middle, jnp.where(lane == 2, low, 0.0))
        )
        inverse = jnp.tile(1.0 / whole, (1, LATENT // 128))
        out_ref[at : at + CHUNK, :LATENT] = (product * inverse).astype(jnp.bfloat16)
        out_ref[at : at + CHUNK, LATENT:] = pieces.astype(jnp.bfloat16)

    old = (old_acc_ref, old_top_ref, old_sum_ref)
    attend(query_ref, place_ref, [keys_ref], old, finish, (ROWS, 2 * ROWS))


def own_kernel(
    query_ref,
    place_ref,
    keys_ref,
    old_acc_ref,
    old_top_ref,
    old_sum_ref,
    acc_ref,
    top_ref,
    sum_ref,
):
    def finish(start, product, top, total):
        acc_ref[start : start + CHUNK, :] = product
        top_ref[start : start + CHUNK, :] = top
        sum_ref[start : start + CHUNK, :] = jnp.broadcast_to(
            jnp.sum(total, axis=1, keepdims=True), (CHUNK, 128)
        )

    old = (old_acc_ref, old_top_ref, old_sum_ref)
    attend(query_ref, place_ref, [keys_ref], old, finish, (0, ROWS))


def merge_kernel(acc_ref, top_ref, sum_ref, got_ref, value_up_ref, out_ref):
    for head in range(HEADS_HERE):
        at = slice(head * TOK, (head + 1) * TOK)
        level = jnp.sum(got_ref[at, LATENT:].astype(jnp.float32), axis=1, keepdims=True)
        level = jnp.broadcast_to(level, (TOK, 128))
        own_top = top_ref[at, :]
        top = jnp.maximum(own_top, level)
        one = jnp.exp2(own_top - top)
        two = jnp.exp2(level - top)
        inverse = 1.0 / (sum_ref[at, :] * one + two)
        one = jnp.tile(one * inverse, (1, LATENT // 128))
        two = jnp.tile(two * inverse, (1, LATENT // 128))
        latent = acc_ref[at, :] * one + got_ref[at, :LATENT].astype(jnp.float32) * two
        out_ref[:, head * VDIM : (head + 1) * VDIM] = jnp.dot(
            latent.astype(jnp.bfloat16), value_up_ref[head], preferred_element_type=jnp.float32
        ).astype(jnp.bfloat16)


def call(kernel, specs, out_shape, name, vmem=32, scratch=()):
    out_specs = jax.tree.map(lambda _: VMEM, out_shape)
    return pl.pallas_call(
        kernel,
        in_specs=specs,
        out_specs=out_specs,
        out_shape=out_shape,
        name=name,
        scratch_shapes=list(scratch),
        compiler_params=pltpu.CompilerParams(vmem_limit_bytes=vmem * 1024 * 1024),
    )


def device_at(y, z, x, c):
    y, z, x = y % NY, z % (NZH * NZL), x % NX
    return (((y * NZH + z // NZL) * NC + c) * NZL + z % NZL) * NX + x


def pairs(target):
    return [
        (device_at(y, z, x, c), device_at(*target(y, z, x, c)))
        for y in range(NY)
        for z in range(NZH * NZL)
        for x in range(NX)
        for c in range(NC)
    ]


def colours():
    return [
        [
            device_at(y, z, x, c)
            for y in range(NY)
            for z in range(NZH * NZL)
            for x in range(NX)
            if (x + y + 2 * z) % 4 == colour
        ]
        for colour in range(4)
        for c in range(NC)
    ]


def shards(query_nope, query_rope, compressed, latent_gain, key_up, value_up, span_order):
    f32 = jnp.float32
    bf16 = jnp.bfloat16
    shape = jax.ShapeDtypeStruct
    frequency = jnp.asarray(FREQUENCY)
    x_pairs = pairs(lambda y, z, x, c: (y, z, x - 1 + 2 * c, c))
    y_pairs = pairs(lambda y, z, x, c: (y + 1 - 2 * c, z, x, 1 - c))
    z_pairs = pairs(lambda y, z, x, c: (y, z - 1 + 2 * c, x, c))
    sibling_pairs = pairs(lambda y, z, x, c: (y, z, x, 1 - c))

    sent = call(
        prep_kernel,
        [HBM] * 4,
        shape((64, 8, WIDE), bf16),
        "prep",
        60,
        [
            pltpu.SMEM((128,), jnp.int32),
            pltpu.VMEM((8, LATENT + ROPE), bf16),
            pltpu.VMEM((1, LATENT), f32),
            pltpu.VMEM((1, 128), f32),
            pltpu.SemaphoreType.DMA((4,)),
        ],
    )(span_order, compressed, latent_gain[None], frequency)
    own_keys = lax.all_to_all(
        sent, AXES, 0, 0, tiled=True, axis_index_groups=colours()
    ).reshape(512, WIDE)
    one = lax.ppermute(own_keys, AXES, x_pairs)
    two = lax.ppermute(own_keys, AXES, y_pairs)
    three = lax.ppermute(own_keys, AXES, z_pairs)
    sibling = lax.ppermute(
        jnp.concatenate([query_nope, query_rope], axis=1), AXES, sibling_pairs
    )
    state = (
        shape((2 * ROWS, LATENT), f32),
        shape((2 * ROWS, 128), f32),
        shape((2 * ROWS, 128), f32),
    )
    queries, places, *carry = call(
        first_kernel,
        [SMEM] + [VMEM] * 6,
        (shape((2 * ROWS, WIDE), bf16), shape((2 * ROWS, 128), f32), *state),
        "first",
    )(span_order, frequency, query_nope, query_rope, sibling, key_up, own_keys)
    carry = call(middle_kernel, [VMEM] * 7, state, "middle")(queries, places, one, two, *carry)
    ending = (queries, places, three, *carry)
    send = call(send_kernel, [VMEM] * 6, shape((ROWS, WIDE), bf16), "sibling_rows")(*ending)
    got = lax.ppermute(send, AXES, sibling_pairs)
    own_state = (
        shape((ROWS, LATENT), f32),
        shape((ROWS, 128), f32),
        shape((ROWS, 128), f32),
    )
    own = call(own_kernel, [VMEM] * 6, own_state, "own_rows")(*ending)
    return call(
        merge_kernel, [VMEM] * 5, shape((TOK, HEADS_HERE * VDIM), bf16), "merge", 16
    )(*own, got, value_up)


def solution(mesh):
    split = Mesh(mesh.devices.reshape(NY, NZH, NC, NZL, NX), AXES)
    placed = (
        P(BLK, HEAD),
        P(BLK, HEAD),
        P(AXES, None),
        P(),
        P(HEAD, None, None),
        P(HEAD, None, None),
        P(),
    )
    return jax.shard_map(
        shards, mesh=split, in_specs=placed, out_specs=P(BLK, HEAD), check_vma=False
    )
```

```python
import functools
import math

import jax
import jax.numpy as jnp
from jax import lax
from jax.experimental import pallas as pl
from jax.experimental.pallas import tpu as pltpu
from jax.sharding import Mesh
from jax.sharding import PartitionSpec as P

AXES = ("y", "zh", "c", "zl", "x")
BLK = ("y", "zh", "c")
HEAD = ("zl", "x")
NY, NZH, NC, NZL, NX = 8, 4, 2, 2, 4

LATENT = 512
ROPE = 64
NOPE = 128
VDIM = 128
HEADS_HERE = 8
TOK = 64
HALF = 32
WIDE = 640
ROWS = TOK * HEADS_HERE
NOPES = HEADS_HERE * NOPE
ROPES = HEADS_HERE * ROPE
JOINED = NOPES + ROPES + 128
CHUNK = 512

norm_epsilon = 1e-06
rope_base = 10000.0
masked_score = -1e30
score_scale = (NOPE + ROPE) ** (-0.5)
log2e = 1.4426950408889634

VMEM = pl.BlockSpec(memory_space=pltpu.VMEM)
SMEM = pl.BlockSpec(memory_space=pltpu.SMEM)
HBM = pl.BlockSpec(memory_space=pltpu.HBM)


def lanes_of(shape):
    return lax.broadcasted_iota(jnp.int32, shape, 1)


def rotation(positions):
    half = ROPE // 2
    lane = lanes_of(positions.shape)
    index = (lane % half).astype(jnp.float32)
    angles = positions * jnp.exp2(index * (-math.log2(rope_base) / half))
    leading = lane % ROPE < half
    sine_value = jnp.sin(angles)
    return jnp.cos(angles), jnp.where(leading, -sine_value, sine_value), leading


def apply_rotation(values, cosine, sine_value, leading):
    swapped = jnp.where(
        leading,
        pltpu.roll(values, 128 - ROPE // 2, 1),
        pltpu.roll(values, ROPE // 2, 1),
    )
    return values * cosine + swapped * sine_value


def block_index():
    return (lax.axis_index("y") * NZH + lax.axis_index("zh")) * NC + lax.axis_index("c")


def prep_kernel(
    span_hbm,
    compressed_hbm,
    gain_hbm,
    nope_hbm,
    rope_hbm,
    out_ref,
    joined_hbm,
    place_ref,
    span_ref,
    compressed_ref,
    gain_ref,
    sems,
):
    copies = [
        pltpu.make_async_copy(source, target, sems.at[k])
        for k, (source, target) in enumerate(
            (
                (compressed_hbm, compressed_ref),
                (gain_hbm, gain_ref),
                (span_hbm, span_ref),
            )
        )
    ]
    joins = [
        pltpu.make_async_copy(source, joined_hbm.at[:, start : start + width], sems.at[3 + k])
        for k, (source, start, width) in enumerate(
            (
                (nope_hbm, 0, NOPES),
                (rope_hbm, NOPES, ROPES),
                (place_ref, NOPES + ROPES, 128),
            )
        )
    ]
    for copy in copies + joins[:2]:
        copy.start()
    for copy in copies:
        copy.wait()
    rows = compressed_ref.shape[0]
    block = block_index()
    x = lax.axis_index("x")
    span = span_ref[block * 2 + lax.axis_index("zl")]
    offset = x * rows + lax.broadcasted_iota(jnp.int32, (rows, 128), 0)
    latent = compressed_ref[:, :LATENT].astype(jnp.float32)
    scale = lax.rsqrt(jnp.mean(latent * latent, axis=1, keepdims=True) + norm_epsilon)
    latent = (latent * scale * gain_ref[...]).astype(jnp.bfloat16)
    rope = compressed_ref[:, LATENT:].astype(jnp.float32)
    rope = jnp.concatenate([rope, jnp.zeros_like(rope)], axis=1)
    positions = (span * HALF + offset).astype(jnp.float32)
    turned = apply_rotation(rope, *rotation(positions))
    lane = lanes_of((rows, 128))
    tail = jnp.where(
        lane < ROPE,
        turned,
        jnp.where(
            lane == ROPE,
            span.astype(jnp.float32),
            jnp.where(lane == ROPE + 1, offset.astype(jnp.float32), 0.0),
        ),
    ).astype(jnp.bfloat16)
    row = jnp.concatenate([latent, tail], axis=1)
    out_ref[...] = jnp.broadcast_to(row[None], out_ref.shape)
    token = lax.broadcasted_iota(jnp.int32, (TOK, 128), 0)
    lane = lanes_of((TOK, 128))
    span = jnp.where(token < HALF, span_ref[block * 2], span_ref[block * 2 + 1])
    place_ref[...] = (
        jnp.where(lane == 0, span, jnp.where(lane == 1, token % HALF, 0))
        .astype(jnp.float32)
        .astype(jnp.bfloat16)
    )
    joins[2].start()
    for copy in joins:
        copy.wait()


def key_positions(keys):
    lane = lanes_of((16, WIDE))
    pick = jnp.where(
        lane == LATENT + ROPE, float(HALF), jnp.where(lane == LATENT + ROPE + 1, 1.0, 0.0)
    ).astype(jnp.bfloat16)
    found = lax.dot_general(
        pick, keys, (((1,), (1,)), ((), ())), preferred_element_type=jnp.float32
    )
    return found[:8]


def query_positions(places):
    row = lax.broadcasted_iota(jnp.int32, (128, 128), 0)
    pick = jnp.where(row == 0, float(HALF), jnp.where(row == 1, 1.0, 0.0)).astype(jnp.bfloat16)
    return jnp.dot(places, pick, preferred_element_type=jnp.float32)


def attend(query_ref, place_ref, key_refs, carry, finish, rows=(0, 2 * ROWS)):
    keys = [ref[...] for ref in key_refs]
    places = [key_positions(block) for block in keys]
    for start in range(*rows, CHUNK):
        queries = query_ref[start : start + CHUNK, :]
        here = place_ref[start : start + CHUNK, :]
        scores = []
        for block, place in zip(keys, places):
            raw = lax.dot_general(
                queries, block, (((1,), (1,)), ((), ())), preferred_element_type=jnp.float32
            )
            pieces = []
            for at in range(0, block.shape[0], 128):
                there = jnp.tile(place[:, at : at + 128], (CHUNK // 8, 1))
                pieces.append(
                    jnp.where(
                        there <= here, raw[:, at : at + 128] * (score_scale * log2e), masked_score
                    )
                )
            scores.append(pieces)
        top = functools.reduce(jnp.maximum, [piece for pieces in scores for piece in pieces])
        top = jnp.broadcast_to(jnp.max(top, axis=1, keepdims=True), (CHUNK, 128))
        if carry is not None:
            old_acc, old_top, old_sum = carry
            before = old_top[start : start + CHUNK, :]
            top = jnp.maximum(top, before)
        product = None
        total = None
        for block, pieces in zip(keys, scores):
            weights = [jnp.exp2(piece - top) for piece in pieces]
            for weight in weights:
                total = weight if total is None else total + weight
            term = jnp.dot(
                jnp.concatenate([weight.astype(jnp.bfloat16) for weight in weights], axis=1),
                block[:, :LATENT],
                preferred_element_type=jnp.float32,
            )
            product = term if product is None else product + term
        if carry is not None:
            shrink = jnp.exp2(before - top)
            product = product + old_acc[start : start + CHUNK, :] * jnp.tile(
                shrink, (1, LATENT // 128)
            )
            total = total + old_sum[start : start + CHUNK, :] * shrink
        finish(start, product, top, total)


def keep(acc_ref, top_ref, sum_ref):
    def finish(start, product, top, total):
        acc_ref[start : start + CHUNK, :] = product
        top_ref[start : start + CHUNK, :] = top
        sum_ref[start : start + CHUNK, :] = total

    return finish


def pair_kernel(own_ref, other_ref, whole_ref):
    rows = own_ref.shape[0]
    whole_ref[:rows, :] = own_ref[...]
    whole_ref[rows:, :] = other_ref[...]


def first_kernel(
    own_ref,
    sibling_ref,
    key_up_ref,
    keys_ref,
    query_ref,
    place_ref,
    acc_ref,
    top_ref,
    sum_ref,
):
    both = jnp.concatenate([own_ref[...], sibling_ref[...]], axis=0)
    nope = both[:, :NOPES]
    rope = both[:, NOPES : NOPES + ROPES]
    positions = query_positions(both[:, NOPES + ROPES :])
    turning = rotation(positions)
    lane = lanes_of((2 * TOK, 128))
    for head in range(HEADS_HERE):
        raised = jnp.dot(
            nope[:, head * NOPE : (head + 1) * NOPE],
            key_up_ref[head],
            preferred_element_type=jnp.float32,
        ).astype(jnp.bfloat16)
        if head % 2 == 0:
            turned = apply_rotation(
                rope[:, head * ROPE : head * ROPE + 128].astype(jnp.float32), *turning
            )
        else:
            turned = pltpu.roll(turned, ROPE, 1)
        tail = jnp.where(lane < ROPE, turned, 0.0).astype(jnp.bfloat16)
        for other in range(2):
            at = other * ROWS + head * TOK
            query_ref[at : at + TOK, :LATENT] = raised[other * TOK : (other + 1) * TOK]
            query_ref[at : at + TOK, LATENT:] = tail[other * TOK : (other + 1) * TOK]
            place_ref[at : at + TOK, :] = positions[other * TOK : (other + 1) * TOK]
    attend(query_ref, place_ref, [keys_ref], None, keep(acc_ref, top_ref, sum_ref))


def middle_kernel(
    query_ref,
    place_ref,
    one_ref,
    two_ref,
    four_ref,
    old_acc_ref,
    old_top_ref,
    old_sum_ref,
    acc_ref,
    top_ref,
    sum_ref,
):
    old = (old_acc_ref, old_top_ref, old_sum_ref)
    attend(
        query_ref, place_ref, [one_ref, two_ref, four_ref], old, keep(acc_ref, top_ref, sum_ref)
    )


def send_kernel(query_ref, place_ref, keys_ref, old_acc_ref, old_top_ref, old_sum_ref, out_ref):
    def finish(start, product, top, total):
        at = start % ROWS
        whole = jnp.broadcast_to(jnp.sum(total, axis=1, keepdims=True), (CHUNK, 128))
        lane = lanes_of((CHUNK, 128))
        level = top + jnp.log2(whole)
        high = level.astype(jnp.bfloat16).astype(jnp.float32)
        rest = level - high
        middle = rest.astype(jnp.bfloat16).astype(jnp.float32)
        low = rest - middle
        pieces = jnp.where(
            lane == 0, high, jnp.where(lane == 1, middle, jnp.where(lane == 2, low, 0.0))
        )
        inverse = jnp.tile(1.0 / whole, (1, LATENT // 128))
        out_ref[at : at + CHUNK, :LATENT] = (product * inverse).astype(jnp.bfloat16)
        out_ref[at : at + CHUNK, LATENT:] = pieces.astype(jnp.bfloat16)

    old = (old_acc_ref, old_top_ref, old_sum_ref)
    attend(query_ref, place_ref, [keys_ref], old, finish, (ROWS, 2 * ROWS))


def own_kernel(
    query_ref,
    place_ref,
    keys_ref,
    old_acc_ref,
    old_top_ref,
    old_sum_ref,
    acc_ref,
    top_ref,
    sum_ref,
):
    def finish(start, product, top, total):
        acc_ref[start : start + CHUNK, :] = product
        top_ref[start : start + CHUNK, :] = top
        sum_ref[start : start + CHUNK, :] = jnp.broadcast_to(
            jnp.sum(total, axis=1, keepdims=True), (CHUNK, 128)
        )

    old = (old_acc_ref, old_top_ref, old_sum_ref)
    attend(query_ref, place_ref, [keys_ref], old, finish, (0, ROWS))


def merge_kernel(acc_ref, top_ref, sum_ref, got_ref, value_up_ref, out_ref):
    for head in range(HEADS_HERE):
        at = slice(head * TOK, (head + 1) * TOK)
        level = jnp.sum(got_ref[at, LATENT:].astype(jnp.float32), axis=1, keepdims=True)
        level = jnp.broadcast_to(level, (TOK, 128))
        own_top = top_ref[at, :]
        top = jnp.maximum(own_top, level)
        one = jnp.exp2(own_top - top)
        two = jnp.exp2(level - top)
        inverse = 1.0 / (sum_ref[at, :] * one + two)
        one = jnp.tile(one * inverse, (1, LATENT // 128))
        two = jnp.tile(two * inverse, (1, LATENT // 128))
        latent = acc_ref[at, :] * one + got_ref[at, :LATENT].astype(jnp.float32) * two
        out_ref[:, head * VDIM : (head + 1) * VDIM] = jnp.dot(
            latent.astype(jnp.bfloat16), value_up_ref[head], preferred_element_type=jnp.float32
        ).astype(jnp.bfloat16)


def call(kernel, specs, out_shape, name, vmem=32, scratch=(), out_specs=None):
    out_specs = out_specs or jax.tree.map(lambda _: VMEM, out_shape)
    return pl.pallas_call(
        kernel,
        in_specs=specs,
        out_specs=out_specs,
        out_shape=out_shape,
        name=name,
        scratch_shapes=list(scratch),
        compiler_params=pltpu.CompilerParams(vmem_limit_bytes=vmem * 1024 * 1024),
    )


def device_at(y, z, x, c):
    y, z, x = y % NY, z % (NZH * NZL), x % NX
    return (((y * NZH + z // NZL) * NC + c) * NZL + z % NZL) * NX + x


def pairs(target):
    return [
        (device_at(y, z, x, c), device_at(*target(y, z, x, c)))
        for y in range(NY)
        for z in range(NZH * NZL)
        for x in range(NX)
        for c in range(NC)
    ]


def colours():
    return [
        [
            device_at(y, z, x, c)
            for y in range(NY)
            for z in range(NZH * NZL)
            for x in range(NX)
            if (2 * x + y + 3 * z) % 8 == colour
        ]
        for colour in range(8)
        for c in range(NC)
    ]


def shards(query_nope, query_rope, compressed, latent_gain, key_up, value_up, span_order):
    f32 = jnp.float32
    bf16 = jnp.bfloat16
    shape = jax.ShapeDtypeStruct
    x_pairs = pairs(lambda y, z, x, c: (y, z, x - 1 + 2 * c, c))
    y_pairs = pairs(lambda y, z, x, c: (y - 1 + 2 * c, z, x, c))
    z_pairs = pairs(lambda y, z, x, c: (y, z - 1 + 2 * c, x, c))
    yz_pairs = pairs(lambda y, z, x, c: (y - 1 + 2 * c, z - 1 + 2 * c, x, c))
    sibling_pairs = pairs(lambda y, z, x, c: (y, z, x, 1 - c))

    sent, joined = call(
        prep_kernel,
        [HBM] * 5,
        (shape((32, 8, WIDE), bf16), shape((TOK, JOINED), bf16)),
        "prep",
        60,
        [
            pltpu.VMEM((TOK, 128), bf16),
            pltpu.SMEM((128,), jnp.int32),
            pltpu.VMEM((8, LATENT + ROPE), bf16),
            pltpu.VMEM((1, LATENT), f32),
            pltpu.SemaphoreType.DMA((6,)),
        ],
        (VMEM, HBM),
    )(span_order, compressed, latent_gain[None], query_nope, query_rope)
    own_keys = lax.all_to_all(
        sent, AXES, 0, 0, tiled=True, axis_index_groups=colours()
    ).reshape(256, WIDE)
    other_half = lax.ppermute(own_keys, AXES, sibling_pairs)
    four = lax.ppermute(own_keys, AXES, yz_pairs)
    whole = call(pair_kernel, [VMEM] * 2, shape((512, WIDE), bf16), "pair", 8)(
        own_keys, other_half
    )
    one = lax.ppermute(whole, AXES, x_pairs)
    two = lax.ppermute(whole, AXES, y_pairs)
    three = lax.ppermute(whole, AXES, z_pairs)
    sibling = lax.ppermute(joined, AXES, sibling_pairs)
    state = (
        shape((2 * ROWS, LATENT), f32),
        shape((2 * ROWS, 128), f32),
        shape((2 * ROWS, 128), f32),
    )
    queries, places, *carry = call(
        first_kernel,
        [VMEM] * 4,
        (shape((2 * ROWS, WIDE), bf16), shape((2 * ROWS, 128), f32), *state),
        "first",
    )(joined, sibling, key_up, own_keys)
    carry = call(middle_kernel, [VMEM] * 8, state, "middle")(
        queries, places, one, two, four, *carry
    )
    ending = (queries, places, three, *carry)
    send = call(send_kernel, [VMEM] * 6, shape((ROWS, WIDE), bf16), "sibling_rows")(*ending)
    got = lax.ppermute(send, AXES, sibling_pairs)
    own_state = (
        shape((ROWS, LATENT), f32),
        shape((ROWS, 128), f32),
        shape((ROWS, 128), f32),
    )
    own = call(own_kernel, [VMEM] * 6, own_state, "own_rows")(*ending)
    return call(
        merge_kernel, [VMEM] * 5, shape((TOK, HEADS_HERE * VDIM), bf16), "merge", 16
    )(*own, got, value_up)


def solution(mesh):
    split = Mesh(mesh.devices.reshape(NY, NZH, NC, NZL, NX), AXES)
    placed = (
        P(BLK, HEAD),
        P(BLK, HEAD),
        P(AXES, None),
        P(),
        P(HEAD, None, None),
        P(HEAD, None, None),
        P(),
    )
    return jax.shard_map(
        shards, mesh=split, in_specs=placed, out_specs=P(BLK, HEAD), check_vma=False
    )
```

```python
import functools
import math

import jax
import jax.numpy as jnp
from jax import lax
from jax.experimental import pallas as pl
from jax.experimental.pallas import tpu as pltpu
from jax.sharding import Mesh
from jax.sharding import PartitionSpec as P

AXES = ("y", "zh", "c", "zl", "x")
BLK = ("y", "zh", "c")
HEAD = ("zl", "x")
NY, NZH, NC, NZL, NX = 8, 4, 2, 2, 4

LATENT = 512
ROPE = 64
NOPE = 128
VDIM = 128
HEADS_HERE = 8
TOK = 64
HALF = 32
WIDE = 640
ROWS = TOK * HEADS_HERE
NOPES = HEADS_HERE * NOPE
ROPES = HEADS_HERE * ROPE
JOINED = NOPES + ROPES + 128
CHUNK = 512

norm_epsilon = 1e-06
rope_base = 10000.0
masked_score = -1e30
score_scale = (NOPE + ROPE) ** (-0.5)
log2e = 1.4426950408889634

VMEM = pl.BlockSpec(memory_space=pltpu.VMEM)
SMEM = pl.BlockSpec(memory_space=pltpu.SMEM)
HBM = pl.BlockSpec(memory_space=pltpu.HBM)


def lanes_of(shape):
    return lax.broadcasted_iota(jnp.int32, shape, 1)


def rotation(positions):
    half = ROPE // 2
    lane = lanes_of(positions.shape)
    index = (lane % half).astype(jnp.float32)
    angles = positions * jnp.exp2(index * (-math.log2(rope_base) / half))
    leading = lane % ROPE < half
    sine_value = jnp.sin(angles)
    return jnp.cos(angles), jnp.where(leading, -sine_value, sine_value), leading


def apply_rotation(values, cosine, sine_value, leading):
    swapped = jnp.where(
        leading,
        pltpu.roll(values, 128 - ROPE // 2, 1),
        pltpu.roll(values, ROPE // 2, 1),
    )
    return values * cosine + swapped * sine_value


def block_index():
    return (lax.axis_index("y") * NZH + lax.axis_index("zh")) * NC + lax.axis_index("c")


def prep_kernel(
    span_hbm,
    compressed_hbm,
    gain_hbm,
    nope_hbm,
    rope_hbm,
    out_ref,
    joined_ref,
    span_ref,
    compressed_ref,
    gain_ref,
    sems,
):
    copies = [
        pltpu.make_async_copy(source, target, sems.at[k])
        for k, (source, target) in enumerate(
            (
                (compressed_hbm, compressed_ref),
                (gain_hbm, gain_ref),
                (span_hbm, span_ref),
            )
        )
    ]
    joins = [
        pltpu.make_async_copy(source, joined_ref.at[:, start : start + width], sems.at[3 + k])
        for k, (source, start, width) in enumerate(
            (
                (nope_hbm, 0, NOPES),
                (rope_hbm, NOPES, ROPES),
            )
        )
    ]
    for copy in copies + joins:
        copy.start()
    for copy in copies:
        copy.wait()
    rows = compressed_ref.shape[0]
    block = block_index()
    x = lax.axis_index("x")
    span = span_ref[block * 2 + lax.axis_index("zl")]
    offset = x * rows + lax.broadcasted_iota(jnp.int32, (rows, 128), 0)
    latent = compressed_ref[:, :LATENT].astype(jnp.float32)
    scale = lax.rsqrt(jnp.mean(latent * latent, axis=1, keepdims=True) + norm_epsilon)
    latent = (latent * scale * gain_ref[...]).astype(jnp.bfloat16)
    rope = compressed_ref[:, LATENT:].astype(jnp.float32)
    rope = jnp.concatenate([rope, jnp.zeros_like(rope)], axis=1)
    positions = (span * HALF + offset).astype(jnp.float32)
    turned = apply_rotation(rope, *rotation(positions))
    lane = lanes_of((rows, 128))
    tail = jnp.where(
        lane < ROPE,
        turned,
        jnp.where(
            lane == ROPE,
            span.astype(jnp.float32),
            jnp.where(lane == ROPE + 1, offset.astype(jnp.float32), 0.0),
        ),
    ).astype(jnp.bfloat16)
    row = jnp.concatenate([latent, tail], axis=1)
    out_ref[...] = jnp.broadcast_to(row[None], out_ref.shape)
    token = lax.broadcasted_iota(jnp.int32, (TOK, 128), 0)
    lane = lanes_of((TOK, 128))
    span = jnp.where(token < HALF, span_ref[block * 2], span_ref[block * 2 + 1])
    joined_ref[:, NOPES + ROPES :] = (
        jnp.where(lane == 0, span, jnp.where(lane == 1, token % HALF, 0))
        .astype(jnp.float32)
        .astype(jnp.bfloat16)
    )
    for copy in joins:
        copy.wait()


def key_positions(keys):
    lane = lanes_of((16, WIDE))
    pick = jnp.where(
        lane == LATENT + ROPE, float(HALF), jnp.where(lane == LATENT + ROPE + 1, 1.0, 0.0)
    ).astype(jnp.bfloat16)
    found = lax.dot_general(
        pick, keys, (((1,), (1,)), ((), ())), preferred_element_type=jnp.float32
    )
    return found[:8]


def query_positions(places):
    row = lax.broadcasted_iota(jnp.int32, (128, 128), 0)
    pick = jnp.where(row == 0, float(HALF), jnp.where(row == 1, 1.0, 0.0)).astype(jnp.bfloat16)
    return jnp.dot(places, pick, preferred_element_type=jnp.float32)


def attend(query_ref, place_ref, key_refs, carry, finish, rows=(0, 2 * ROWS)):
    keys = [ref[...] for ref in key_refs]
    places = [key_positions(block) for block in keys]
    for start in range(*rows, CHUNK):
        queries = query_ref[start : start + CHUNK, :]
        here = place_ref[start : start + CHUNK, :]
        scores = []
        for block, place in zip(keys, places):
            raw = lax.dot_general(
                queries, block, (((1,), (1,)), ((), ())), preferred_element_type=jnp.float32
            )
            pieces = []
            for at in range(0, block.shape[0], 128):
                there = jnp.tile(place[:, at : at + 128], (CHUNK // 8, 1))
                pieces.append(
                    jnp.where(
                        there <= here, raw[:, at : at + 128] * (score_scale * log2e), masked_score
                    )
                )
            scores.append(pieces)
        top = functools.reduce(jnp.maximum, [piece for pieces in scores for piece in pieces])
        top = jnp.broadcast_to(jnp.max(top, axis=1, keepdims=True), (CHUNK, 128))
        if carry is not None:
            old_acc, old_top, old_sum = carry
            before = old_top[start : start + CHUNK, :]
            top = jnp.maximum(top, before)
        product = None
        total = None
        for block, pieces in zip(keys, scores):
            weights = [jnp.exp2(piece - top) for piece in pieces]
            for weight in weights:
                total = weight if total is None else total + weight
            term = jnp.dot(
                jnp.concatenate([weight.astype(jnp.bfloat16) for weight in weights], axis=1),
                block[:, :LATENT],
                preferred_element_type=jnp.float32,
            )
            product = term if product is None else product + term
        if carry is not None:
            shrink = jnp.exp2(before - top)
            product = product + old_acc[start : start + CHUNK, :] * jnp.tile(
                shrink, (1, LATENT // 128)
            )
            total = total + old_sum[start : start + CHUNK, :] * shrink
        finish(start, product, top, total)


def keep(acc_ref, top_ref, sum_ref):
    def finish(start, product, top, total):
        acc_ref[start : start + CHUNK, :] = product
        top_ref[start : start + CHUNK, :] = top
        sum_ref[start : start + CHUNK, :] = total

    return finish


def pair_kernel(own_ref, other_ref, whole_ref):
    rows = own_ref.shape[0]
    whole_ref[:rows, :] = own_ref[...]
    whole_ref[rows:, :] = other_ref[...]


def first_kernel(
    own_ref,
    sibling_ref,
    key_up_ref,
    keys_ref,
    query_ref,
    place_ref,
    acc_ref,
    top_ref,
    sum_ref,
):
    both = jnp.concatenate([own_ref[...], sibling_ref[...]], axis=0)
    nope = both[:, :NOPES]
    rope = both[:, NOPES : NOPES + ROPES]
    positions = query_positions(both[:, NOPES + ROPES :])
    turning = rotation(positions)
    lane = lanes_of((2 * TOK, 128))
    for head in range(HEADS_HERE):
        raised = jnp.dot(
            nope[:, head * NOPE : (head + 1) * NOPE],
            key_up_ref[head],
            preferred_element_type=jnp.float32,
        ).astype(jnp.bfloat16)
        if head % 2 == 0:
            turned = apply_rotation(
                rope[:, head * ROPE : head * ROPE + 128].astype(jnp.float32), *turning
            )
        else:
            turned = pltpu.roll(turned, ROPE, 1)
        tail = jnp.where(lane < ROPE, turned, 0.0).astype(jnp.bfloat16)
        for other in range(2):
            at = other * ROWS + head * TOK
            query_ref[at : at + TOK, :LATENT] = raised[other * TOK : (other + 1) * TOK]
            query_ref[at : at + TOK, LATENT:] = tail[other * TOK : (other + 1) * TOK]
            place_ref[at : at + TOK, :] = positions[other * TOK : (other + 1) * TOK]
    attend(query_ref, place_ref, [keys_ref], None, keep(acc_ref, top_ref, sum_ref))


def middle_kernel(
    query_ref,
    place_ref,
    one_ref,
    two_ref,
    old_acc_ref,
    old_top_ref,
    old_sum_ref,
    acc_ref,
    top_ref,
    sum_ref,
):
    old = (old_acc_ref, old_top_ref, old_sum_ref)
    attend(query_ref, place_ref, [one_ref, two_ref], old, keep(acc_ref, top_ref, sum_ref))


def send_kernel(
    query_ref, place_ref, keys_ref, four_ref, old_acc_ref, old_top_ref, old_sum_ref, out_ref
):
    def finish(start, product, top, total):
        at = start % ROWS
        whole = jnp.broadcast_to(jnp.sum(total, axis=1, keepdims=True), (CHUNK, 128))
        lane = lanes_of((CHUNK, 128))
        level = top + jnp.log2(whole)
        high = level.astype(jnp.bfloat16).astype(jnp.float32)
        rest = level - high
        middle = rest.astype(jnp.bfloat16).astype(jnp.float32)
        low = rest - middle
        pieces = jnp.where(
            lane == 0, high, jnp.where(lane == 1, middle, jnp.where(lane == 2, low, 0.0))
        )
        inverse = jnp.tile(1.0 / whole, (1, LATENT // 128))
        out_ref[at : at + CHUNK, :LATENT] = (product * inverse).astype(jnp.bfloat16)
        out_ref[at : at + CHUNK, LATENT:] = pieces.astype(jnp.bfloat16)

    old = (old_acc_ref, old_top_ref, old_sum_ref)
    attend(query_ref, place_ref, [keys_ref, four_ref], old, finish, (ROWS, 2 * ROWS))


def own_kernel(
    query_ref,
    place_ref,
    keys_ref,
    four_ref,
    old_acc_ref,
    old_top_ref,
    old_sum_ref,
    acc_ref,
    top_ref,
    sum_ref,
):
    def finish(start, product, top, total):
        acc_ref[start : start + CHUNK, :] = product
        top_ref[start : start + CHUNK, :] = top
        sum_ref[start : start + CHUNK, :] = jnp.broadcast_to(
            jnp.sum(total, axis=1, keepdims=True), (CHUNK, 128)
        )

    old = (old_acc_ref, old_top_ref, old_sum_ref)
    attend(query_ref, place_ref, [keys_ref, four_ref], old, finish, (0, ROWS))


def merge_kernel(acc_ref, top_ref, sum_ref, got_ref, value_up_ref, out_ref):
    for head in range(HEADS_HERE):
        at = slice(head * TOK, (head + 1) * TOK)
        level = jnp.sum(got_ref[at, LATENT:].astype(jnp.float32), axis=1, keepdims=True)
        level = jnp.broadcast_to(level, (TOK, 128))
        own_top = top_ref[at, :]
        top = jnp.maximum(own_top, level)
        one = jnp.exp2(own_top - top)
        two = jnp.exp2(level - top)
        inverse = 1.0 / (sum_ref[at, :] * one + two)
        one = jnp.tile(one * inverse, (1, LATENT // 128))
        two = jnp.tile(two * inverse, (1, LATENT // 128))
        latent = acc_ref[at, :] * one + got_ref[at, :LATENT].astype(jnp.float32) * two
        out_ref[:, head * VDIM : (head + 1) * VDIM] = jnp.dot(
            latent.astype(jnp.bfloat16), value_up_ref[head], preferred_element_type=jnp.float32
        ).astype(jnp.bfloat16)


def call(kernel, specs, out_shape, name, vmem=32, scratch=(), out_specs=None):
    out_specs = out_specs or jax.tree.map(lambda _: VMEM, out_shape)
    return pl.pallas_call(
        kernel,
        in_specs=specs,
        out_specs=out_specs,
        out_shape=out_shape,
        name=name,
        scratch_shapes=list(scratch),
        compiler_params=pltpu.CompilerParams(vmem_limit_bytes=vmem * 1024 * 1024),
    )


def device_at(y, z, x, c):
    y, z, x = y % NY, z % (NZH * NZL), x % NX
    return (((y * NZH + z // NZL) * NC + c) * NZL + z % NZL) * NX + x


def pairs(target):
    return [
        (device_at(y, z, x, c), device_at(*target(y, z, x, c)))
        for y in range(NY)
        for z in range(NZH * NZL)
        for x in range(NX)
        for c in range(NC)
    ]


def colours():
    return [
        [
            device_at(y, z, x, c)
            for y in range(NY)
            for z in range(NZH * NZL)
            for x in range(NX)
            if (2 * x + y + 3 * z) % 8 == colour
        ]
        for colour in range(8)
        for c in range(NC)
    ]


def shards(query_nope, query_rope, compressed, latent_gain, key_up, value_up, span_order):
    f32 = jnp.float32
    bf16 = jnp.bfloat16
    shape = jax.ShapeDtypeStruct
    x_pairs = pairs(lambda y, z, x, c: (y, z, x - 1 + 2 * c, c))
    y_pairs = pairs(lambda y, z, x, c: (y - 1 + 2 * c, z, x, c))
    z_pairs = pairs(lambda y, z, x, c: (y, z - 1 + 2 * c, x, c))
    yz_pairs = pairs(lambda y, z, x, c: (y - 1 + 2 * c, z - 1 + 2 * c, x, c))
    sibling_pairs = pairs(lambda y, z, x, c: (y, z, x, 1 - c))

    sent, joined = call(
        prep_kernel,
        [HBM] * 5,
        (shape((32, 8, WIDE), bf16), shape((TOK, JOINED), bf16)),
        "prep",
        60,
        [
            pltpu.SMEM((128,), jnp.int32),
            pltpu.VMEM((8, LATENT + ROPE), bf16),
            pltpu.VMEM((1, LATENT), f32),
            pltpu.SemaphoreType.DMA((5,)),
        ],
    )(span_order, compressed, latent_gain[None], query_nope, query_rope)
    own_keys = lax.all_to_all(
        sent, AXES, 0, 0, tiled=True, axis_index_groups=colours()
    ).reshape(256, WIDE)
    other_half = lax.ppermute(own_keys, AXES, sibling_pairs)
    sibling = lax.ppermute(joined, AXES, sibling_pairs)
    other_half, sibling = lax.optimization_barrier((other_half, sibling))
    four = lax.ppermute(own_keys, AXES, yz_pairs)
    whole = call(pair_kernel, [VMEM] * 2, shape((512, WIDE), bf16), "pair", 8)(
        own_keys, other_half
    )
    one = lax.ppermute(whole, AXES, x_pairs)
    two = lax.ppermute(whole, AXES, y_pairs)
    three = lax.ppermute(whole, AXES, z_pairs)
    state = (
        shape((2 * ROWS, LATENT), f32),
        shape((2 * ROWS, 128), f32),
        shape((2 * ROWS, 128), f32),
    )
    queries, places, *carry = call(
        first_kernel,
        [VMEM] * 4,
        (shape((2 * ROWS, WIDE), bf16), shape((2 * ROWS, 128), f32), *state),
        "first",
    )(joined, sibling, key_up, own_keys)
    carry = call(middle_kernel, [VMEM] * 7, state, "middle")(queries, places, one, two, *carry)
    ending = (queries, places, three, four, *carry)
    send = call(send_kernel, [VMEM] * 7, shape((ROWS, WIDE), bf16), "sibling_rows")(*ending)
    got = lax.ppermute(send, AXES, sibling_pairs)
    own_state = (
        shape((ROWS, LATENT), f32),
        shape((ROWS, 128), f32),
        shape((ROWS, 128), f32),
    )
    own = call(own_kernel, [VMEM] * 7, own_state, "own_rows")(*ending)
    return call(
        merge_kernel, [VMEM] * 5, shape((TOK, HEADS_HERE * VDIM), bf16), "merge", 16
    )(*own, got, value_up)


def solution(mesh):
    split = Mesh(mesh.devices.reshape(NY, NZH, NC, NZL, NX), AXES)
    placed = (
        P(BLK, HEAD),
        P(BLK, HEAD),
        P(AXES, None),
        P(),
        P(HEAD, None, None),
        P(HEAD, None, None),
        P(),
    )
    return jax.shard_map(
        shards, mesh=split, in_specs=placed, out_specs=P(BLK, HEAD), check_vma=False
    )
```

```python
import functools
import math

import jax
import jax.numpy as jnp
from jax import lax
from jax.experimental import pallas as pl
from jax.experimental.pallas import tpu as pltpu
from jax.sharding import Mesh
from jax.sharding import PartitionSpec as P

AXES = ("y", "zh", "c", "zl", "x")
BLK = ("y", "zh", "c")
HEAD = ("zl", "x")
NY, NZH, NC, NZL, NX = 8, 4, 2, 2, 4

LATENT = 512
ROPE = 64
NOPE = 128
VDIM = 128
HEADS_HERE = 8
TOK = 64
HALF = 32
WIDE = 640
ROWS = TOK * HEADS_HERE
NOPES = HEADS_HERE * NOPE
ROPES = HEADS_HERE * ROPE
JOINED = NOPES + ROPES + 128
CHUNK = 512

norm_epsilon = 1e-06
rope_base = 10000.0
masked_score = -1e30
score_scale = (NOPE + ROPE) ** (-0.5)
log2e = 1.4426950408889634

VMEM = pl.BlockSpec(memory_space=pltpu.VMEM)
SMEM = pl.BlockSpec(memory_space=pltpu.SMEM)
HBM = pl.BlockSpec(memory_space=pltpu.HBM)


def lanes_of(shape):
    return lax.broadcasted_iota(jnp.int32, shape, 1)


def rotation(positions):
    half = ROPE // 2
    lane = lanes_of(positions.shape)
    index = (lane % half).astype(jnp.float32)
    angles = positions * jnp.exp2(index * (-math.log2(rope_base) / half))
    leading = lane % ROPE < half
    sine_value = jnp.sin(angles)
    return jnp.cos(angles), jnp.where(leading, -sine_value, sine_value), leading


def apply_rotation(values, cosine, sine_value, leading):
    swapped = jnp.where(
        leading,
        pltpu.roll(values, 128 - ROPE // 2, 1),
        pltpu.roll(values, ROPE // 2, 1),
    )
    return values * cosine + swapped * sine_value


def block_index():
    return (lax.axis_index("y") * NZH + lax.axis_index("zh")) * NC + lax.axis_index("c")


def prep_kernel(
    span_hbm,
    compressed_hbm,
    gain_hbm,
    nope_hbm,
    rope_hbm,
    out_ref,
    joined_ref,
    span_ref,
    compressed_ref,
    gain_ref,
    sems,
):
    copies = [
        pltpu.make_async_copy(source, target, sems.at[k])
        for k, (source, target) in enumerate(
            (
                (compressed_hbm, compressed_ref),
                (gain_hbm, gain_ref),
                (span_hbm, span_ref),
            )
        )
    ]
    joins = [
        pltpu.make_async_copy(source, joined_ref.at[:, start : start + width], sems.at[3 + k])
        for k, (source, start, width) in enumerate(
            (
                (nope_hbm, 0, NOPES),
                (rope_hbm, NOPES, ROPES),
            )
        )
    ]
    for copy in copies + joins:
        copy.start()
    for copy in copies:
        copy.wait()
    rows = compressed_ref.shape[0]
    block = block_index()
    x = lax.axis_index("x")
    span = span_ref[block * 2 + lax.axis_index("zl")]
    offset = x * rows + lax.broadcasted_iota(jnp.int32, (rows, 128), 0)
    latent = compressed_ref[:, :LATENT].astype(jnp.float32)
    scale = lax.rsqrt(jnp.mean(latent * latent, axis=1, keepdims=True) + norm_epsilon)
    latent = (latent * scale * gain_ref[...]).astype(jnp.bfloat16)
    rope = compressed_ref[:, LATENT:].astype(jnp.float32)
    rope = jnp.concatenate([rope, jnp.zeros_like(rope)], axis=1)
    positions = (span * HALF + offset).astype(jnp.float32)
    turned = apply_rotation(rope, *rotation(positions))
    lane = lanes_of((rows, 128))
    tail = jnp.where(
        lane < ROPE,
        turned,
        jnp.where(
            lane == ROPE,
            span.astype(jnp.float32),
            jnp.where(lane == ROPE + 1, offset.astype(jnp.float32), 0.0),
        ),
    ).astype(jnp.bfloat16)
    row = jnp.concatenate([latent, tail], axis=1)
    out_ref[...] = jnp.broadcast_to(row[None], out_ref.shape)
    token = lax.broadcasted_iota(jnp.int32, (TOK, 128), 0)
    lane = lanes_of((TOK, 128))
    span = jnp.where(token < HALF, span_ref[block * 2], span_ref[block * 2 + 1])
    joined_ref[:, NOPES + ROPES :] = (
        jnp.where(lane == 0, span, jnp.where(lane == 1, token % HALF, 0))
        .astype(jnp.float32)
        .astype(jnp.bfloat16)
    )
    for copy in joins:
        copy.wait()


def position_rows():
    lane = lanes_of((16, WIDE))
    return jnp.where(
        lane == LATENT + ROPE, float(HALF), jnp.where(lane == LATENT + ROPE + 1, 1.0, 0.0)
    ).astype(jnp.bfloat16)


def query_positions(places):
    row = lax.broadcasted_iota(jnp.int32, (128, 128), 0)
    pick = jnp.where(row == 0, float(HALF), jnp.where(row == 1, 1.0, 0.0)).astype(jnp.bfloat16)
    return jnp.dot(places, pick, preferred_element_type=jnp.float32)


def attend(query_ref, place_ref, key_refs, carry, finish, rows=(0, 2 * ROWS)):
    keys = [ref[...] for ref in key_refs]
    places = [None] * len(keys)
    for start in range(*rows, CHUNK):
        queries = query_ref[start : start + CHUNK, :]
        if start == rows[0]:
            queries = jnp.concatenate([queries, position_rows()], axis=0)
        here = place_ref[start : start + CHUNK, :]
        scores = []
        for k, block in enumerate(keys):
            raw = lax.dot_general(
                queries, block, (((1,), (1,)), ((), ())), preferred_element_type=jnp.float32
            )
            if start == rows[0]:
                places[k] = raw[CHUNK : CHUNK + 8]
                raw = raw[:CHUNK]
            place = places[k]
            pieces = []
            for at in range(0, block.shape[0], 128):
                there = jnp.tile(place[:, at : at + 128], (CHUNK // 8, 1))
                pieces.append(
                    jnp.where(
                        there <= here, raw[:, at : at + 128] * (score_scale * log2e), masked_score
                    )
                )
            scores.append(pieces)
        top = functools.reduce(jnp.maximum, [piece for pieces in scores for piece in pieces])
        top = jnp.broadcast_to(jnp.max(top, axis=1, keepdims=True), (CHUNK, 128))
        if carry is not None:
            old_acc, old_top, old_sum = carry
            before = old_top[start : start + CHUNK, :]
            top = jnp.maximum(top, before)
        product = None
        total = None
        for block, pieces in zip(keys, scores):
            weights = [jnp.exp2(piece - top) for piece in pieces]
            for weight in weights:
                total = weight if total is None else total + weight
            term = jnp.dot(
                jnp.concatenate([weight.astype(jnp.bfloat16) for weight in weights], axis=1),
                block[:, :LATENT],
                preferred_element_type=jnp.float32,
            )
            product = term if product is None else product + term
        if carry is not None:
            shrink = jnp.exp2(before - top)
            product = product + old_acc[start : start + CHUNK, :] * jnp.tile(
                shrink, (1, LATENT // 128)
            )
            total = total + old_sum[start : start + CHUNK, :] * shrink
        finish(start, product, top, total)


def keep(acc_ref, top_ref, sum_ref):
    def finish(start, product, top, total):
        acc_ref[start : start + CHUNK, :] = product
        top_ref[start : start + CHUNK, :] = top
        sum_ref[start : start + CHUNK, :] = total

    return finish


def first_kernel(
    own_ref,
    sibling_ref,
    key_up_ref,
    keys_ref,
    query_ref,
    place_ref,
    acc_ref,
    top_ref,
    sum_ref,
):
    both = jnp.concatenate([own_ref[...], sibling_ref[...]], axis=0)
    nope = both[:, :NOPES]
    rope = both[:, NOPES : NOPES + ROPES]
    positions = query_positions(both[:, NOPES + ROPES :])
    turning = rotation(positions)
    lane = lanes_of((2 * TOK, 128))
    for head in range(HEADS_HERE):
        raised = jnp.dot(
            nope[:, head * NOPE : (head + 1) * NOPE],
            key_up_ref[head],
            preferred_element_type=jnp.float32,
        ).astype(jnp.bfloat16)
        if head % 2 == 0:
            turned = apply_rotation(
                rope[:, head * ROPE : head * ROPE + 128].astype(jnp.float32), *turning
            )
        else:
            turned = pltpu.roll(turned, ROPE, 1)
        tail = jnp.where(lane < ROPE, turned, 0.0).astype(jnp.bfloat16)
        for other in range(2):
            at = other * ROWS + head * TOK
            query_ref[at : at + TOK, :LATENT] = raised[other * TOK : (other + 1) * TOK]
            query_ref[at : at + TOK, LATENT:] = tail[other * TOK : (other + 1) * TOK]
            place_ref[at : at + TOK, :] = positions[other * TOK : (other + 1) * TOK]
    attend(query_ref, place_ref, [keys_ref], None, keep(acc_ref, top_ref, sum_ref))


def middle_kernel(
    query_ref,
    place_ref,
    one_ref,
    two_ref,
    old_acc_ref,
    old_top_ref,
    old_sum_ref,
    acc_ref,
    top_ref,
    sum_ref,
):
    old = (old_acc_ref, old_top_ref, old_sum_ref)
    attend(query_ref, place_ref, [one_ref, two_ref], old, keep(acc_ref, top_ref, sum_ref))


def send_kernel(
    query_ref, place_ref, keys_ref, old_acc_ref, old_top_ref, old_sum_ref, out_ref
):
    def finish(start, product, top, total):
        at = start % ROWS
        whole = jnp.broadcast_to(jnp.sum(total, axis=1, keepdims=True), (CHUNK, 128))
        lane = lanes_of((CHUNK, 128))
        level = top + jnp.log2(whole)
        high = level.astype(jnp.bfloat16).astype(jnp.float32)
        rest = level - high
        middle = rest.astype(jnp.bfloat16).astype(jnp.float32)
        low = rest - middle
        pieces = jnp.where(
            lane == 0, high, jnp.where(lane == 1, middle, jnp.where(lane == 2, low, 0.0))
        )
        inverse = jnp.tile(1.0 / whole, (1, LATENT // 128))
        out_ref[at : at + CHUNK, :LATENT] = (product * inverse).astype(jnp.bfloat16)
        out_ref[at : at + CHUNK, LATENT:] = pieces.astype(jnp.bfloat16)

    old = (old_acc_ref, old_top_ref, old_sum_ref)
    attend(query_ref, place_ref, [keys_ref], old, finish, (ROWS, 2 * ROWS))


def own_kernel(
    query_ref,
    place_ref,
    keys_ref,
    old_acc_ref,
    old_top_ref,
    old_sum_ref,
    acc_ref,
    top_ref,
    sum_ref,
):
    def finish(start, product, top, total):
        acc_ref[start : start + CHUNK, :] = product
        top_ref[start : start + CHUNK, :] = top
        sum_ref[start : start + CHUNK, :] = jnp.broadcast_to(
            jnp.sum(total, axis=1, keepdims=True), (CHUNK, 128)
        )

    old = (old_acc_ref, old_top_ref, old_sum_ref)
    attend(query_ref, place_ref, [keys_ref], old, finish, (0, ROWS))


def merge_kernel(acc_ref, top_ref, sum_ref, got_ref, value_up_ref, out_ref):
    for head in range(HEADS_HERE):
        at = slice(head * TOK, (head + 1) * TOK)
        level = jnp.sum(got_ref[at, LATENT:].astype(jnp.float32), axis=1, keepdims=True)
        level = jnp.broadcast_to(level, (TOK, 128))
        own_top = top_ref[at, :]
        top = jnp.maximum(own_top, level)
        one = jnp.exp2(own_top - top)
        two = jnp.exp2(level - top)
        inverse = 1.0 / (sum_ref[at, :] * one + two)
        one = jnp.tile(one * inverse, (1, LATENT // 128))
        two = jnp.tile(two * inverse, (1, LATENT // 128))
        latent = acc_ref[at, :] * one + got_ref[at, :LATENT].astype(jnp.float32) * two
        out_ref[:, head * VDIM : (head + 1) * VDIM] = jnp.dot(
            latent.astype(jnp.bfloat16), value_up_ref[head], preferred_element_type=jnp.float32
        ).astype(jnp.bfloat16)


def call(kernel, specs, out_shape, name, vmem=32, scratch=(), out_specs=None):
    out_specs = out_specs or jax.tree.map(lambda _: VMEM, out_shape)
    return pl.pallas_call(
        kernel,
        in_specs=specs,
        out_specs=out_specs,
        out_shape=out_shape,
        name=name,
        scratch_shapes=list(scratch),
        compiler_params=pltpu.CompilerParams(vmem_limit_bytes=vmem * 1024 * 1024),
    )


def device_at(y, z, x, c):
    y, z, x = y % NY, z % (NZH * NZL), x % NX
    return (((y * NZH + z // NZL) * NC + c) * NZL + z % NZL) * NX + x


def pairs(target):
    return [
        (device_at(y, z, x, c), device_at(*target(y, z, x, c)))
        for y in range(NY)
        for z in range(NZH * NZL)
        for x in range(NX)
        for c in range(NC)
    ]


def colours():
    return [
        [
            device_at(y, z, x, c)
            for y in range(NY)
            for z in range(NZH * NZL)
            for x in range(NX)
            if (x + y + 2 * z) % 4 == colour
        ]
        for colour in range(4)
        for c in range(NC)
    ]


def shards(query_nope, query_rope, compressed, latent_gain, key_up, value_up, span_order):
    f32 = jnp.float32
    bf16 = jnp.bfloat16
    shape = jax.ShapeDtypeStruct
    x_pairs = pairs(lambda y, z, x, c: (y, z, x - 1 + 2 * c, c))
    y_pairs = pairs(lambda y, z, x, c: (y + 1 - 2 * c, z, x, 1 - c))
    z_pairs = pairs(lambda y, z, x, c: (y, z - 1 + 2 * c, x, c))
    sibling_pairs = pairs(lambda y, z, x, c: (y, z, x, 1 - c))

    sent, joined = call(
        prep_kernel,
        [HBM] * 5,
        (shape((64, 8, WIDE), bf16), shape((TOK, JOINED), bf16)),
        "prep",
        60,
        [
            pltpu.SMEM((128,), jnp.int32),
            pltpu.VMEM((8, LATENT + ROPE), bf16),
            pltpu.VMEM((1, LATENT), f32),
            pltpu.SemaphoreType.DMA((5,)),
        ],
    )(span_order, compressed, latent_gain[None], query_nope, query_rope)
    own_keys = lax.all_to_all(
        sent, AXES, 0, 0, tiled=True, axis_index_groups=colours()
    ).reshape(512, WIDE)
    one = lax.ppermute(own_keys, AXES, x_pairs)
    two = lax.ppermute(own_keys, AXES, y_pairs)
    three = lax.ppermute(own_keys, AXES, z_pairs)
    sibling = lax.ppermute(joined, AXES, sibling_pairs)
    state = (
        shape((2 * ROWS, LATENT), f32),
        shape((2 * ROWS, 128), f32),
        shape((2 * ROWS, 128), f32),
    )
    queries, places, *carry = call(
        first_kernel,
        [VMEM] * 4,
        (shape((2 * ROWS, WIDE), bf16), shape((2 * ROWS, 128), f32), *state),
        "first",
    )(joined, sibling, key_up, own_keys)
    carry = call(middle_kernel, [VMEM] * 7, state, "middle")(queries, places, one, two, *carry)
    ending = (queries, places, three, *carry)
    send = call(send_kernel, [VMEM] * 6, shape((ROWS, WIDE), bf16), "sibling_rows")(*ending)
    got = lax.ppermute(send, AXES, sibling_pairs)
    own_state = (
        shape((ROWS, LATENT), f32),
        shape((ROWS, 128), f32),
        shape((ROWS, 128), f32),
    )
    own = call(own_kernel, [VMEM] * 6, own_state, "own_rows")(*ending)
    return call(
        merge_kernel, [VMEM] * 5, shape((TOK, HEADS_HERE * VDIM), bf16), "merge", 16
    )(*own, got, value_up)


def solution(mesh):
    split = Mesh(mesh.devices.reshape(NY, NZH, NC, NZL, NX), AXES)
    placed = (
        P(BLK, HEAD),
        P(BLK, HEAD),
        P(AXES, None),
        P(),
        P(HEAD, None, None),
        P(HEAD, None, None),
        P(),
    )
    return jax.shard_map(
        shards, mesh=split, in_specs=placed, out_specs=P(BLK, HEAD), check_vma=False
    )
```

```python
import functools
import math

import jax
import jax.numpy as jnp
from jax import lax
from jax.experimental import pallas as pl
from jax.experimental.pallas import tpu as pltpu
from jax.sharding import Mesh
from jax.sharding import PartitionSpec as P

AXES = ("y", "zh", "c", "zl", "x")
BLK = ("y", "zh", "c")
HEAD = ("zl", "x")
NY, NZH, NC, NZL, NX = 8, 4, 2, 2, 4

LATENT = 512
ROPE = 64
NOPE = 128
VDIM = 128
HEADS_HERE = 8
TOK = 64
HALF = 32
WIDE = 640
ROWS = TOK * HEADS_HERE
NOPES = HEADS_HERE * NOPE
ROPES = HEADS_HERE * ROPE
JOINED = NOPES + ROPES + 128
CHUNK = 512

norm_epsilon = 1e-06
rope_base = 10000.0
masked_score = -1e30
score_scale = (NOPE + ROPE) ** (-0.5)
log2e = 1.4426950408889634

VMEM = pl.BlockSpec(memory_space=pltpu.VMEM)
SMEM = pl.BlockSpec(memory_space=pltpu.SMEM)
HBM = pl.BlockSpec(memory_space=pltpu.HBM)


def lanes_of(shape):
    return lax.broadcasted_iota(jnp.int32, shape, 1)


def rotation(positions):
    half = ROPE // 2
    lane = lanes_of(positions.shape)
    index = (lane % half).astype(jnp.float32)
    angles = positions * jnp.exp2(index * (-math.log2(rope_base) / half))
    leading = lane % ROPE < half
    sine_value = jnp.sin(angles)
    return jnp.cos(angles), jnp.where(leading, -sine_value, sine_value), leading


def apply_rotation(values, cosine, sine_value, leading):
    swapped = jnp.where(
        leading,
        pltpu.roll(values, 128 - ROPE // 2, 1),
        pltpu.roll(values, ROPE // 2, 1),
    )
    return values * cosine + swapped * sine_value


def block_index():
    return (lax.axis_index("y") * NZH + lax.axis_index("zh")) * NC + lax.axis_index("c")


def prep_kernel(
    span_hbm,
    compressed_hbm,
    gain_hbm,
    nope_hbm,
    rope_hbm,
    out_ref,
    joined_ref,
    span_ref,
    compressed_ref,
    gain_ref,
    sems,
):
    copies = [
        pltpu.make_async_copy(source, target, sems.at[k])
        for k, (source, target) in enumerate(
            (
                (compressed_hbm, compressed_ref),
                (gain_hbm, gain_ref),
                (span_hbm, span_ref),
            )
        )
    ]
    joins = [
        pltpu.make_async_copy(source, joined_ref.at[:, start : start + width], sems.at[3 + k])
        for k, (source, start, width) in enumerate(
            (
                (nope_hbm, 0, NOPES),
                (rope_hbm, NOPES, ROPES),
            )
        )
    ]
    for copy in copies + joins:
        copy.start()
    for copy in copies:
        copy.wait()
    rows = compressed_ref.shape[0]
    block = block_index()
    x = lax.axis_index("x")
    span = span_ref[block * 2 + lax.axis_index("zl")]
    offset = x * rows + lax.broadcasted_iota(jnp.int32, (rows, 128), 0)
    latent = compressed_ref[:, :LATENT].astype(jnp.float32)
    scale = lax.rsqrt(jnp.mean(latent * latent, axis=1, keepdims=True) + norm_epsilon)
    latent = (latent * scale * gain_ref[...]).astype(jnp.bfloat16)
    rope = compressed_ref[:, LATENT:].astype(jnp.float32)
    rope = jnp.concatenate([rope, jnp.zeros_like(rope)], axis=1)
    positions = (span * HALF + offset).astype(jnp.float32)
    turned = apply_rotation(rope, *rotation(positions))
    lane = lanes_of((rows, 128))
    tail = jnp.where(
        lane < ROPE,
        turned,
        jnp.where(
            lane == ROPE,
            span.astype(jnp.float32),
            jnp.where(lane == ROPE + 1, offset.astype(jnp.float32), 0.0),
        ),
    ).astype(jnp.bfloat16)
    row = jnp.concatenate([latent, tail], axis=1)
    out_ref[...] = jnp.broadcast_to(row[None], out_ref.shape)
    token = lax.broadcasted_iota(jnp.int32, (TOK, 128), 0)
    lane = lanes_of((TOK, 128))
    span = jnp.where(token < HALF, span_ref[block * 2], span_ref[block * 2 + 1])
    joined_ref[:, NOPES + ROPES :] = (
        jnp.where(lane == 0, span, jnp.where(lane == 1, token % HALF, 0))
        .astype(jnp.float32)
        .astype(jnp.bfloat16)
    )
    for copy in joins:
        copy.wait()


def position_rows():
    lane = lanes_of((16, WIDE))
    return jnp.where(
        lane == LATENT + ROPE, float(HALF), jnp.where(lane == LATENT + ROPE + 1, 1.0, 0.0)
    ).astype(jnp.bfloat16)


def query_positions(places):
    row = lax.broadcasted_iota(jnp.int32, (128, 128), 0)
    pick = jnp.where(row == 0, float(HALF), jnp.where(row == 1, 1.0, 0.0)).astype(jnp.bfloat16)
    return jnp.dot(places, pick, preferred_element_type=jnp.float32)


def attend(query_ref, place_ref, key_refs, carry, finish, rows=(0, ROWS)):
    keys = [ref[...] for ref in key_refs]
    places = [None] * len(keys)
    for start in range(*rows, CHUNK):
        queries = query_ref[start : start + CHUNK, :]
        if start == rows[0]:
            queries = jnp.concatenate([queries, position_rows()], axis=0)
        here = place_ref[start : start + CHUNK, :]
        scores = []
        for k, block in enumerate(keys):
            raw = lax.dot_general(
                queries, block, (((1,), (1,)), ((), ())), preferred_element_type=jnp.float32
            )
            if start == rows[0]:
                places[k] = raw[CHUNK : CHUNK + 8]
                raw = raw[:CHUNK]
            place = places[k]
            pieces = []
            for at in range(0, block.shape[0], 128):
                there = jnp.tile(place[:, at : at + 128], (CHUNK // 8, 1))
                pieces.append(
                    jnp.where(
                        there <= here, raw[:, at : at + 128] * (score_scale * log2e), masked_score
                    )
                )
            scores.append(pieces)
        top = functools.reduce(jnp.maximum, [piece for pieces in scores for piece in pieces])
        top = jnp.broadcast_to(jnp.max(top, axis=1, keepdims=True), (CHUNK, 128))
        if carry is not None:
            old_acc, old_top, old_sum = carry
            before = old_top[start : start + CHUNK, :]
            top = jnp.maximum(top, before)
        product = None
        total = None
        for block, pieces in zip(keys, scores):
            weights = [jnp.exp2(piece - top) for piece in pieces]
            for weight in weights:
                total = weight if total is None else total + weight
            term = jnp.dot(
                jnp.concatenate([weight.astype(jnp.bfloat16) for weight in weights], axis=1),
                block[:, :LATENT],
                preferred_element_type=jnp.float32,
            )
            product = term if product is None else product + term
        if carry is not None:
            shrink = jnp.exp2(before - top)
            product = product + old_acc[start : start + CHUNK, :] * jnp.tile(
                shrink, (1, LATENT // 128)
            )
            total = total + old_sum[start : start + CHUNK, :] * shrink
        finish(start, product, top, total)


def keep(acc_ref, top_ref, sum_ref):
    def finish(start, product, top, total):
        acc_ref[start : start + CHUNK, :] = product
        top_ref[start : start + CHUNK, :] = top
        sum_ref[start : start + CHUNK, :] = total

    return finish


def project(joined_ref, key_up_ref, query_ref, place_ref):
    joined = joined_ref[...]
    positions = query_positions(joined[:, NOPES + ROPES :])
    turning = rotation(positions)
    lane = lanes_of((TOK, 128))
    for head in range(HEADS_HERE):
        at = slice(head * TOK, (head + 1) * TOK)
        query_ref[at, :LATENT] = jnp.dot(
            joined[:, head * NOPE : (head + 1) * NOPE],
            key_up_ref[head],
            preferred_element_type=jnp.float32,
        ).astype(jnp.bfloat16)
        if head % 2 == 0:
            first = NOPES + head * ROPE
            turned = apply_rotation(joined[:, first : first + 128].astype(jnp.float32), *turning)
        else:
            turned = pltpu.roll(turned, ROPE, 1)
        query_ref[at, LATENT:] = jnp.where(lane < ROPE, turned, 0.0).astype(jnp.bfloat16)
        place_ref[at, :] = positions


def first_kernel(
    own_ref, key_up_ref, keys_ref, query_ref, place_ref, acc_ref, top_ref, sum_ref
):
    project(own_ref, key_up_ref, query_ref, place_ref)
    attend(query_ref, place_ref, [keys_ref], None, keep(acc_ref, top_ref, sum_ref))


def middle_kernel(
    query_ref,
    place_ref,
    sibling_ref,
    key_up_ref,
    keys_ref,
    one_ref,
    two_ref,
    old_acc_ref,
    old_top_ref,
    old_sum_ref,
    acc_ref,
    top_ref,
    sum_ref,
    sibling_query_ref,
    sibling_place_ref,
    sibling_acc_ref,
    sibling_top_ref,
    sibling_sum_ref,
):
    project(sibling_ref, key_up_ref, sibling_query_ref, sibling_place_ref)
    old = (old_acc_ref, old_top_ref, old_sum_ref)
    attend(query_ref, place_ref, [one_ref, two_ref], old, keep(acc_ref, top_ref, sum_ref))
    attend(
        sibling_query_ref,
        sibling_place_ref,
        [keys_ref, one_ref, two_ref],
        None,
        keep(sibling_acc_ref, sibling_top_ref, sibling_sum_ref),
    )


def send_kernel(
    query_ref, place_ref, keys_ref, old_acc_ref, old_top_ref, old_sum_ref, out_ref
):
    def finish(start, product, top, total):
        at = start % ROWS
        whole = jnp.broadcast_to(jnp.sum(total, axis=1, keepdims=True), (CHUNK, 128))
        lane = lanes_of((CHUNK, 128))
        level = top + jnp.log2(whole)
        high = level.astype(jnp.bfloat16).astype(jnp.float32)
        rest = level - high
        middle = rest.astype(jnp.bfloat16).astype(jnp.float32)
        low = rest - middle
        pieces = jnp.where(
            lane == 0, high, jnp.where(lane == 1, middle, jnp.where(lane == 2, low, 0.0))
        )
        inverse = jnp.tile(1.0 / whole, (1, LATENT // 128))
        out_ref[at : at + CHUNK, :LATENT] = (product * inverse).astype(jnp.bfloat16)
        out_ref[at : at + CHUNK, LATENT:] = pieces.astype(jnp.bfloat16)

    old = (old_acc_ref, old_top_ref, old_sum_ref)
    attend(query_ref, place_ref, [keys_ref], old, finish)


def own_kernel(
    query_ref,
    place_ref,
    keys_ref,
    old_acc_ref,
    old_top_ref,
    old_sum_ref,
    acc_ref,
    top_ref,
    sum_ref,
):
    def finish(start, product, top, total):
        acc_ref[start : start + CHUNK, :] = product
        top_ref[start : start + CHUNK, :] = top
        sum_ref[start : start + CHUNK, :] = jnp.broadcast_to(
            jnp.sum(total, axis=1, keepdims=True), (CHUNK, 128)
        )

    old = (old_acc_ref, old_top_ref, old_sum_ref)
    attend(query_ref, place_ref, [keys_ref], old, finish)


def merge_kernel(acc_ref, top_ref, sum_ref, got_ref, value_up_ref, out_ref):
    for head in range(HEADS_HERE):
        at = slice(head * TOK, (head + 1) * TOK)
        level = jnp.sum(got_ref[at, LATENT:].astype(jnp.float32), axis=1, keepdims=True)
        level = jnp.broadcast_to(level, (TOK, 128))
        own_top = top_ref[at, :]
        top = jnp.maximum(own_top, level)
        one = jnp.exp2(own_top - top)
        two = jnp.exp2(level - top)
        inverse = 1.0 / (sum_ref[at, :] * one + two)
        one = jnp.tile(one * inverse, (1, LATENT // 128))
        two = jnp.tile(two * inverse, (1, LATENT // 128))
        latent = acc_ref[at, :] * one + got_ref[at, :LATENT].astype(jnp.float32) * two
        out_ref[:, head * VDIM : (head + 1) * VDIM] = jnp.dot(
            latent.astype(jnp.bfloat16), value_up_ref[head], preferred_element_type=jnp.float32
        ).astype(jnp.bfloat16)


def call(kernel, specs, out_shape, name, vmem=32, scratch=(), out_specs=None):
    out_specs = out_specs or jax.tree.map(lambda _: VMEM, out_shape)
    return pl.pallas_call(
        kernel,
        in_specs=specs,
        out_specs=out_specs,
        out_shape=out_shape,
        name=name,
        scratch_shapes=list(scratch),
        compiler_params=pltpu.CompilerParams(vmem_limit_bytes=vmem * 1024 * 1024),
    )


def device_at(y, z, x, c):
    y, z, x = y % NY, z % (NZH * NZL), x % NX
    return (((y * NZH + z // NZL) * NC + c) * NZL + z % NZL) * NX + x


def pairs(target):
    return [
        (device_at(y, z, x, c), device_at(*target(y, z, x, c)))
        for y in range(NY)
        for z in range(NZH * NZL)
        for x in range(NX)
        for c in range(NC)
    ]


def colours():
    return [
        [
            device_at(y, z, x, c)
            for y in range(NY)
            for z in range(NZH * NZL)
            for x in range(NX)
            if (x + y + 2 * z) % 4 == colour
        ]
        for colour in range(4)
        for c in range(NC)
    ]


def shards(query_nope, query_rope, compressed, latent_gain, key_up, value_up, span_order):
    f32 = jnp.float32
    bf16 = jnp.bfloat16
    shape = jax.ShapeDtypeStruct
    x_pairs = pairs(lambda y, z, x, c: (y, z, x - 1 + 2 * c, c))
    y_pairs = pairs(lambda y, z, x, c: (y + 1 - 2 * c, z, x, 1 - c))
    z_pairs = pairs(lambda y, z, x, c: (y, z - 1 + 2 * c, x, c))
    sibling_pairs = pairs(lambda y, z, x, c: (y, z, x, 1 - c))

    sent, joined = call(
        prep_kernel,
        [HBM] * 5,
        (shape((64, 8, WIDE), bf16), shape((TOK, JOINED), bf16)),
        "prep",
        60,
        [
            pltpu.SMEM((128,), jnp.int32),
            pltpu.VMEM((8, LATENT + ROPE), bf16),
            pltpu.VMEM((1, LATENT), f32),
            pltpu.SemaphoreType.DMA((5,)),
        ],
    )(span_order, compressed, latent_gain[None], query_nope, query_rope)
    own_keys = lax.all_to_all(
        sent, AXES, 0, 0, tiled=True, axis_index_groups=colours()
    ).reshape(512, WIDE)
    one = lax.ppermute(own_keys, AXES, x_pairs)
    two = lax.ppermute(own_keys, AXES, y_pairs)
    three = lax.ppermute(own_keys, AXES, z_pairs)
    sibling = lax.ppermute(joined, AXES, sibling_pairs)
    state = (shape((ROWS, LATENT), f32), shape((ROWS, 128), f32), shape((ROWS, 128), f32))
    rows = (shape((ROWS, WIDE), bf16), shape((ROWS, 128), f32))
    queries, places, *carry = call(first_kernel, [VMEM] * 3, (*rows, *state), "first")(
        joined, key_up, own_keys
    )
    *carry, acc, top, total = call(middle_kernel, [VMEM] * 10, (*state, *rows, *state), "middle")(
        queries, places, sibling, key_up, own_keys, one, two, *carry
    )
    *carry, sibling_queries, sibling_places = carry
    send = call(send_kernel, [VMEM] * 6, shape((ROWS, WIDE), bf16), "sibling_rows")(
        sibling_queries, sibling_places, three, acc, top, total
    )
    got = lax.ppermute(send, AXES, sibling_pairs)
    own = call(own_kernel, [VMEM] * 6, state, "own_rows")(queries, places, three, *carry)
    return call(
        merge_kernel, [VMEM] * 5, shape((TOK, HEADS_HERE * VDIM), bf16), "merge", 16
    )(*own, got, value_up)


def solution(mesh):
    split = Mesh(mesh.devices.reshape(NY, NZH, NC, NZL, NX), AXES)
    placed = (
        P(BLK, HEAD),
        P(BLK, HEAD),
        P(AXES, None),
        P(),
        P(HEAD, None, None),
        P(HEAD, None, None),
        P(),
    )
    return jax.shard_map(
        shards, mesh=split, in_specs=placed, out_specs=P(BLK, HEAD), check_vma=False
    )
```

```python
import functools
import math

import jax
import jax.numpy as jnp
from jax import lax
from jax.experimental import pallas as pl
from jax.experimental.pallas import tpu as pltpu
from jax.sharding import Mesh
from jax.sharding import PartitionSpec as P

AXES = ("y", "zh", "c", "zl", "x")
BLK = ("y", "zh", "c")
HEAD = ("zl", "x")
NY, NZH, NC, NZL, NX = 8, 4, 2, 2, 4

LATENT = 512
ROPE = 64
NOPE = 128
VDIM = 128
HEADS_HERE = 8
TOK = 64
HALF = 32
WIDE = 640
ROWS = TOK * HEADS_HERE
NOPES = HEADS_HERE * NOPE
ROPES = HEADS_HERE * ROPE
JOINED = NOPES + ROPES + 128
CHUNK = 512

norm_epsilon = 1e-06
rope_base = 10000.0
masked_score = -1e30
score_scale = (NOPE + ROPE) ** (-0.5)
log2e = 1.4426950408889634

VMEM = pl.BlockSpec(memory_space=pltpu.VMEM)
SMEM = pl.BlockSpec(memory_space=pltpu.SMEM)
HBM = pl.BlockSpec(memory_space=pltpu.HBM)


def lanes_of(shape):
    return lax.broadcasted_iota(jnp.int32, shape, 1)


def rotation(positions):
    half = ROPE // 2
    lane = lanes_of(positions.shape)
    index = (lane % half).astype(jnp.float32)
    angles = positions * jnp.exp2(index * (-math.log2(rope_base) / half))
    leading = lane % ROPE < half
    sine_value = jnp.sin(angles)
    return jnp.cos(angles), jnp.where(leading, -sine_value, sine_value), leading


def apply_rotation(values, cosine, sine_value, leading):
    swapped = jnp.where(
        leading,
        pltpu.roll(values, 128 - ROPE // 2, 1),
        pltpu.roll(values, ROPE // 2, 1),
    )
    return values * cosine + swapped * sine_value


def block_index():
    return (lax.axis_index("y") * NZH + lax.axis_index("zh")) * NC + lax.axis_index("c")


def prep_kernel(
    span_hbm,
    compressed_hbm,
    gain_hbm,
    nope_hbm,
    rope_hbm,
    out_ref,
    joined_ref,
    span_ref,
    compressed_ref,
    gain_ref,
    sems,
):
    copies = [
        pltpu.make_async_copy(source, target, sems.at[k])
        for k, (source, target) in enumerate(
            (
                (compressed_hbm, compressed_ref),
                (gain_hbm, gain_ref),
                (span_hbm, span_ref),
            )
        )
    ]
    joins = [
        pltpu.make_async_copy(source, joined_ref.at[:, start : start + width], sems.at[3 + k])
        for k, (source, start, width) in enumerate(
            (
                (nope_hbm, 0, NOPES),
                (rope_hbm, NOPES, ROPES),
            )
        )
    ]
    for copy in copies + joins:
        copy.start()
    for copy in copies:
        copy.wait()
    rows = compressed_ref.shape[0]
    block = block_index()
    x = lax.axis_index("x")
    span = span_ref[block * 2 + lax.axis_index("zl")]
    offset = x * rows + lax.broadcasted_iota(jnp.int32, (rows, 128), 0)
    latent = compressed_ref[:, :LATENT].astype(jnp.float32)
    scale = lax.rsqrt(jnp.mean(latent * latent, axis=1, keepdims=True) + norm_epsilon)
    latent = (latent * scale * gain_ref[...]).astype(jnp.bfloat16)
    rope = compressed_ref[:, LATENT:].astype(jnp.float32)
    rope = jnp.concatenate([rope, jnp.zeros_like(rope)], axis=1)
    positions = (span * HALF + offset).astype(jnp.float32)
    turned = apply_rotation(rope, *rotation(positions))
    lane = lanes_of((rows, 128))
    tail = jnp.where(
        lane < ROPE,
        turned,
        jnp.where(
            lane == ROPE,
            span.astype(jnp.float32),
            jnp.where(lane == ROPE + 1, offset.astype(jnp.float32), 0.0),
        ),
    ).astype(jnp.bfloat16)
    row = jnp.concatenate([latent, tail], axis=1)
    out_ref[...] = jnp.broadcast_to(row[None], out_ref.shape)
    token = lax.broadcasted_iota(jnp.int32, (TOK, 128), 0)
    lane = lanes_of((TOK, 128))
    span = jnp.where(token < HALF, span_ref[block * 2], span_ref[block * 2 + 1])
    joined_ref[:, NOPES + ROPES :] = (
        jnp.where(lane == 0, span, jnp.where(lane == 1, token % HALF, 0))
        .astype(jnp.float32)
        .astype(jnp.bfloat16)
    )
    for copy in joins:
        copy.wait()


def position_rows():
    lane = lanes_of((16, WIDE))
    return jnp.where(
        lane == LATENT + ROPE, float(HALF), jnp.where(lane == LATENT + ROPE + 1, 1.0, 0.0)
    ).astype(jnp.bfloat16)


def query_positions(places):
    row = lax.broadcasted_iota(jnp.int32, (128, 128), 0)
    pick = jnp.where(row == 0, float(HALF), jnp.where(row == 1, 1.0, 0.0)).astype(jnp.bfloat16)
    return jnp.dot(places, pick, preferred_element_type=jnp.float32)


def attend(query_ref, place_ref, key_refs, carry, finish, rows=(0, ROWS)):
    keys = [ref[...] for ref in key_refs]
    places = [None] * len(keys)
    for start in range(*rows, CHUNK):
        queries = query_ref[start : start + CHUNK, :]
        if start == rows[0]:
            queries = jnp.concatenate([queries, position_rows()], axis=0)
        here = place_ref[start : start + CHUNK, :]
        scores = []
        for k, block in enumerate(keys):
            raw = lax.dot_general(
                queries, block, (((1,), (1,)), ((), ())), preferred_element_type=jnp.float32
            )
            if start == rows[0]:
                places[k] = raw[CHUNK : CHUNK + 8]
                raw = raw[:CHUNK]
            place = places[k]
            pieces = []
            for at in range(0, block.shape[0], 128):
                there = jnp.tile(place[:, at : at + 128], (CHUNK // 8, 1))
                pieces.append(
                    jnp.where(
                        there <= here, raw[:, at : at + 128] * (score_scale * log2e), masked_score
                    )
                )
            scores.append(pieces)
        top = functools.reduce(jnp.maximum, [piece for pieces in scores for piece in pieces])
        top = jnp.broadcast_to(jnp.max(top, axis=1, keepdims=True), (CHUNK, 128))
        if carry is not None:
            old_acc, old_top, old_sum = carry
            before = old_top[start : start + CHUNK, :]
            top = jnp.maximum(top, before)
        product = None
        total = None
        for block, pieces in zip(keys, scores):
            weights = [jnp.exp2(piece - top) for piece in pieces]
            for weight in weights:
                total = weight if total is None else total + weight
            term = jnp.dot(
                jnp.concatenate([weight.astype(jnp.bfloat16) for weight in weights], axis=1),
                block[:, :LATENT],
                preferred_element_type=jnp.float32,
            )
            product = term if product is None else product + term
        if carry is not None:
            shrink = jnp.exp2(before - top)
            product = product + old_acc[start : start + CHUNK, :] * jnp.tile(
                shrink, (1, LATENT // 128)
            )
            total = total + old_sum[start : start + CHUNK, :] * shrink
        finish(start, product, top, total)


def keep(acc_ref, top_ref, sum_ref):
    def finish(start, product, top, total):
        acc_ref[start : start + CHUNK, :] = product
        top_ref[start : start + CHUNK, :] = top
        sum_ref[start : start + CHUNK, :] = total

    return finish


def project(joined_ref, key_up_ref, query_ref, place_ref):
    joined = joined_ref[...]
    positions = query_positions(joined[:, NOPES + ROPES :])
    turning = rotation(positions)
    lane = lanes_of((TOK, 128))
    for head in range(HEADS_HERE):
        at = slice(head * TOK, (head + 1) * TOK)
        query_ref[at, :LATENT] = jnp.dot(
            joined[:, head * NOPE : (head + 1) * NOPE],
            key_up_ref[head],
            preferred_element_type=jnp.float32,
        ).astype(jnp.bfloat16)
        if head % 2 == 0:
            first = NOPES + head * ROPE
            turned = apply_rotation(joined[:, first : first + 128].astype(jnp.float32), *turning)
        else:
            turned = pltpu.roll(turned, ROPE, 1)
        query_ref[at, LATENT:] = jnp.where(lane < ROPE, turned, 0.0).astype(jnp.bfloat16)
        place_ref[at, :] = positions


def first_kernel(
    own_ref, key_up_ref, keys_ref, query_ref, place_ref, acc_ref, top_ref, sum_ref
):
    project(own_ref, key_up_ref, query_ref, place_ref)
    attend(query_ref, place_ref, [keys_ref], None, keep(acc_ref, top_ref, sum_ref))


def middle_kernel(one_ref, two_ref, *refs):
    for side in range(2):
        query_ref, place_ref, *old = refs[side * 5 : side * 5 + 5]
        new = refs[10 + side * 3 : 13 + side * 3]
        attend(query_ref, place_ref, [one_ref, two_ref], old, keep(*new))


def send_kernel(
    query_ref, place_ref, keys_ref, old_acc_ref, old_top_ref, old_sum_ref, out_ref
):
    def finish(start, product, top, total):
        at = start % ROWS
        whole = jnp.broadcast_to(jnp.sum(total, axis=1, keepdims=True), (CHUNK, 128))
        lane = lanes_of((CHUNK, 128))
        level = top + jnp.log2(whole)
        high = level.astype(jnp.bfloat16).astype(jnp.float32)
        rest = level - high
        middle = rest.astype(jnp.bfloat16).astype(jnp.float32)
        low = rest - middle
        pieces = jnp.where(
            lane == 0, high, jnp.where(lane == 1, middle, jnp.where(lane == 2, low, 0.0))
        )
        inverse = jnp.tile(1.0 / whole, (1, LATENT // 128))
        out_ref[at : at + CHUNK, :LATENT] = (product * inverse).astype(jnp.bfloat16)
        out_ref[at : at + CHUNK, LATENT:] = pieces.astype(jnp.bfloat16)

    old = (old_acc_ref, old_top_ref, old_sum_ref)
    attend(query_ref, place_ref, [keys_ref], old, finish)


def own_kernel(
    query_ref,
    place_ref,
    keys_ref,
    old_acc_ref,
    old_top_ref,
    old_sum_ref,
    acc_ref,
    top_ref,
    sum_ref,
):
    def finish(start, product, top, total):
        acc_ref[start : start + CHUNK, :] = product
        top_ref[start : start + CHUNK, :] = top
        sum_ref[start : start + CHUNK, :] = jnp.broadcast_to(
            jnp.sum(total, axis=1, keepdims=True), (CHUNK, 128)
        )

    old = (old_acc_ref, old_top_ref, old_sum_ref)
    attend(query_ref, place_ref, [keys_ref], old, finish)


def merge_kernel(acc_ref, top_ref, sum_ref, got_ref, value_up_ref, out_ref):
    for head in range(HEADS_HERE):
        at = slice(head * TOK, (head + 1) * TOK)
        level = jnp.sum(got_ref[at, LATENT:].astype(jnp.float32), axis=1, keepdims=True)
        level = jnp.broadcast_to(level, (TOK, 128))
        own_top = top_ref[at, :]
        top = jnp.maximum(own_top, level)
        one = jnp.exp2(own_top - top)
        two = jnp.exp2(level - top)
        inverse = 1.0 / (sum_ref[at, :] * one + two)
        one = jnp.tile(one * inverse, (1, LATENT // 128))
        two = jnp.tile(two * inverse, (1, LATENT // 128))
        latent = acc_ref[at, :] * one + got_ref[at, :LATENT].astype(jnp.float32) * two
        out_ref[:, head * VDIM : (head + 1) * VDIM] = jnp.dot(
            latent.astype(jnp.bfloat16), value_up_ref[head], preferred_element_type=jnp.float32
        ).astype(jnp.bfloat16)


def call(kernel, specs, out_shape, name, vmem=32, scratch=(), out_specs=None):
    out_specs = out_specs or jax.tree.map(lambda _: VMEM, out_shape)
    return pl.pallas_call(
        kernel,
        in_specs=specs,
        out_specs=out_specs,
        out_shape=out_shape,
        name=name,
        scratch_shapes=list(scratch),
        compiler_params=pltpu.CompilerParams(vmem_limit_bytes=vmem * 1024 * 1024),
    )


def device_at(y, z, x, c):
    y, z, x = y % NY, z % (NZH * NZL), x % NX
    return (((y * NZH + z // NZL) * NC + c) * NZL + z % NZL) * NX + x


def pairs(target):
    return [
        (device_at(y, z, x, c), device_at(*target(y, z, x, c)))
        for y in range(NY)
        for z in range(NZH * NZL)
        for x in range(NX)
        for c in range(NC)
    ]


def colours():
    return [
        [
            device_at(y, z, x, c)
            for y in range(NY)
            for z in range(NZH * NZL)
            for x in range(NX)
            if (x + y + 2 * z) % 4 == colour
        ]
        for colour in range(4)
        for c in range(NC)
    ]


def shards(query_nope, query_rope, compressed, latent_gain, key_up, value_up, span_order):
    f32 = jnp.float32
    bf16 = jnp.bfloat16
    shape = jax.ShapeDtypeStruct
    x_pairs = pairs(lambda y, z, x, c: (y, z, x - 1 + 2 * c, c))
    y_pairs = pairs(lambda y, z, x, c: (y + 1 - 2 * c, z, x, 1 - c))
    z_pairs = pairs(lambda y, z, x, c: (y, z - 1 + 2 * c, x, c))
    sibling_pairs = pairs(lambda y, z, x, c: (y, z, x, 1 - c))

    sent, joined = call(
        prep_kernel,
        [HBM] * 5,
        (shape((64, 8, WIDE), bf16), shape((TOK, JOINED), bf16)),
        "prep",
        60,
        [
            pltpu.SMEM((128,), jnp.int32),
            pltpu.VMEM((8, LATENT + ROPE), bf16),
            pltpu.VMEM((1, LATENT), f32),
            pltpu.SemaphoreType.DMA((5,)),
        ],
    )(span_order, compressed, latent_gain[None], query_nope, query_rope)
    own_keys = lax.all_to_all(
        sent, AXES, 0, 0, tiled=True, axis_index_groups=colours()
    ).reshape(512, WIDE)
    one = lax.ppermute(own_keys, AXES, x_pairs)
    two = lax.ppermute(own_keys, AXES, y_pairs)
    three = lax.ppermute(own_keys, AXES, z_pairs)
    sibling = lax.ppermute(joined, AXES, sibling_pairs)
    state = (shape((ROWS, LATENT), f32), shape((ROWS, 128), f32), shape((ROWS, 128), f32))
    rows = (shape((ROWS, WIDE), bf16), shape((ROWS, 128), f32))
    first = call(first_kernel, [VMEM] * 3, (*rows, *state), "first")
    here = first(joined, key_up, own_keys)
    there = first(sibling, key_up, own_keys)
    carry = call(middle_kernel, [VMEM] * 12, (*state, *state), "middle")(one, two, *here, *there)
    send = call(send_kernel, [VMEM] * 6, shape((ROWS, WIDE), bf16), "sibling_rows")(
        *there[:2], three, *carry[3:]
    )
    got = lax.ppermute(send, AXES, sibling_pairs)
    own = call(own_kernel, [VMEM] * 6, state, "own_rows")(*here[:2], three, *carry[:3])
    return call(
        merge_kernel, [VMEM] * 5, shape((TOK, HEADS_HERE * VDIM), bf16), "merge", 16
    )(*own, got, value_up)


def solution(mesh):
    split = Mesh(mesh.devices.reshape(NY, NZH, NC, NZL, NX), AXES)
    placed = (
        P(BLK, HEAD),
        P(BLK, HEAD),
        P(AXES, None),
        P(),
        P(HEAD, None, None),
        P(HEAD, None, None),
        P(),
    )
    return jax.shard_map(
        shards, mesh=split, in_specs=placed, out_specs=P(BLK, HEAD), check_vma=False
    )
```

```python
import functools
import math

import jax
import jax.numpy as jnp
from jax import lax
from jax.experimental import pallas as pl
from jax.experimental.pallas import tpu as pltpu
from jax.sharding import Mesh
from jax.sharding import PartitionSpec as P

AXES = ("y", "zh", "c", "zl", "x")
BLK = ("y", "zh", "c")
HEAD = ("zl", "x")
NY, NZH, NC, NZL, NX = 8, 4, 2, 2, 4

LATENT = 512
ROPE = 64
NOPE = 128
VDIM = 128
HEADS_HERE = 8
TOK = 64
HALF = 32
WIDE = 640
ROWS = TOK * HEADS_HERE
NOPES = HEADS_HERE * NOPE
ROPES = HEADS_HERE * ROPE
JOINED = NOPES + ROPES + 128
CHUNK = 512

norm_epsilon = 1e-06
rope_base = 10000.0
masked_score = -1e30
score_scale = (NOPE + ROPE) ** (-0.5)
log2e = 1.4426950408889634

VMEM = pl.BlockSpec(memory_space=pltpu.VMEM)
SMEM = pl.BlockSpec(memory_space=pltpu.SMEM)
HBM = pl.BlockSpec(memory_space=pltpu.HBM)


def lanes_of(shape):
    return lax.broadcasted_iota(jnp.int32, shape, 1)


def rotation(positions):
    half = ROPE // 2
    lane = lanes_of(positions.shape)
    index = (lane % half).astype(jnp.float32)
    angles = positions * jnp.exp2(index * (-math.log2(rope_base) / half))
    leading = lane % ROPE < half
    sine_value = jnp.sin(angles)
    return jnp.cos(angles), jnp.where(leading, -sine_value, sine_value), leading


def apply_rotation(values, cosine, sine_value, leading):
    swapped = jnp.where(
        leading,
        pltpu.roll(values, 128 - ROPE // 2, 1),
        pltpu.roll(values, ROPE // 2, 1),
    )
    return values * cosine + swapped * sine_value


def block_index():
    return (lax.axis_index("y") * NZH + lax.axis_index("zh")) * NC + lax.axis_index("c")


def prep_kernel(
    span_hbm,
    compressed_hbm,
    gain_hbm,
    nope_hbm,
    rope_hbm,
    out_ref,
    joined_ref,
    span_ref,
    compressed_ref,
    gain_ref,
    sems,
):
    copies = [
        pltpu.make_async_copy(source, target, sems.at[k])
        for k, (source, target) in enumerate(
            (
                (compressed_hbm, compressed_ref),
                (gain_hbm, gain_ref),
                (span_hbm, span_ref),
            )
        )
    ]
    joins = [
        pltpu.make_async_copy(source, joined_ref.at[:, start : start + width], sems.at[3 + k])
        for k, (source, start, width) in enumerate(
            (
                (nope_hbm, 0, NOPES),
                (rope_hbm, NOPES, ROPES),
            )
        )
    ]
    for copy in copies + joins:
        copy.start()
    for copy in copies:
        copy.wait()
    rows = compressed_ref.shape[0]
    block = block_index()
    x = lax.axis_index("x")
    span = span_ref[block * 2 + lax.axis_index("zl")]
    offset = x * rows + lax.broadcasted_iota(jnp.int32, (rows, 128), 0)
    latent = compressed_ref[:, :LATENT].astype(jnp.float32)
    scale = lax.rsqrt(jnp.mean(latent * latent, axis=1, keepdims=True) + norm_epsilon)
    latent = (latent * scale * gain_ref[...]).astype(jnp.bfloat16)
    rope = compressed_ref[:, LATENT:].astype(jnp.float32)
    rope = jnp.concatenate([rope, jnp.zeros_like(rope)], axis=1)
    positions = (span * HALF + offset).astype(jnp.float32)
    turned = apply_rotation(rope, *rotation(positions))
    lane = lanes_of((rows, 128))
    tail = jnp.where(
        lane < ROPE,
        turned,
        jnp.where(
            lane == ROPE,
            span.astype(jnp.float32),
            jnp.where(lane == ROPE + 1, offset.astype(jnp.float32), 0.0),
        ),
    ).astype(jnp.bfloat16)
    row = jnp.concatenate([latent, tail], axis=1)
    out_ref[...] = jnp.broadcast_to(row[None], out_ref.shape)
    token = lax.broadcasted_iota(jnp.int32, (TOK, 128), 0)
    lane = lanes_of((TOK, 128))
    span = jnp.where(token < HALF, span_ref[block * 2], span_ref[block * 2 + 1])
    joined_ref[:, NOPES + ROPES :] = (
        jnp.where(lane == 0, span, jnp.where(lane == 1, token % HALF, 0))
        .astype(jnp.float32)
        .astype(jnp.bfloat16)
    )
    for copy in joins:
        copy.wait()


def position_rows():
    lane = lanes_of((16, WIDE))
    return jnp.where(
        lane == LATENT + ROPE, float(HALF), jnp.where(lane == LATENT + ROPE + 1, 1.0, 0.0)
    ).astype(jnp.bfloat16)


def query_positions(places):
    row = lax.broadcasted_iota(jnp.int32, (128, 128), 0)
    pick = jnp.where(row == 0, float(HALF), jnp.where(row == 1, 1.0, 0.0)).astype(jnp.bfloat16)
    return jnp.dot(places, pick, preferred_element_type=jnp.float32)


def attend(query_ref, place_ref, key_refs, carry, finish, rows=(0, ROWS)):
    keys = [ref[...] for ref in key_refs]
    places = [None] * len(keys)
    for start in range(*rows, CHUNK):
        queries = query_ref[start : start + CHUNK, :]
        if start == rows[0]:
            queries = jnp.concatenate([queries, position_rows()], axis=0)
        here = place_ref[start : start + CHUNK, :]
        scores = []
        for k, block in enumerate(keys):
            raw = lax.dot_general(
                queries, block, (((1,), (1,)), ((), ())), preferred_element_type=jnp.float32
            )
            if start == rows[0]:
                places[k] = raw[CHUNK : CHUNK + 8]
                raw = raw[:CHUNK]
            place = places[k]
            pieces = []
            for at in range(0, block.shape[0], 128):
                there = jnp.tile(place[:, at : at + 128], (CHUNK // 8, 1))
                pieces.append(
                    jnp.where(
                        there <= here, raw[:, at : at + 128] * (score_scale * log2e), masked_score
                    )
                )
            scores.append(pieces)
        top = functools.reduce(jnp.maximum, [piece for pieces in scores for piece in pieces])
        top = jnp.broadcast_to(jnp.max(top, axis=1, keepdims=True), (CHUNK, 128))
        if carry is not None:
            old_acc, old_top, old_sum = carry
            before = old_top[start : start + CHUNK, :]
            top = jnp.maximum(top, before)
        product = None
        total = None
        for block, pieces in zip(keys, scores):
            weights = [jnp.exp2(piece - top) for piece in pieces]
            for weight in weights:
                total = weight if total is None else total + weight
            term = jnp.dot(
                jnp.concatenate([weight.astype(jnp.bfloat16) for weight in weights], axis=1),
                block[:, :LATENT],
                preferred_element_type=jnp.float32,
            )
            product = term if product is None else product + term
        if carry is not None:
            shrink = jnp.exp2(before - top)
            product = product + old_acc[start : start + CHUNK, :] * jnp.tile(
                shrink, (1, LATENT // 128)
            )
            total = total + old_sum[start : start + CHUNK, :] * shrink
        finish(start, product, top, total)


def keep(acc_ref, top_ref, sum_ref):
    def finish(start, product, top, total):
        acc_ref[start : start + CHUNK, :] = product
        top_ref[start : start + CHUNK, :] = top
        sum_ref[start : start + CHUNK, :] = total

    return finish


def project(joined_ref, key_up_ref, query_ref, place_ref):
    joined = joined_ref[...]
    positions = query_positions(joined[:, NOPES + ROPES :])
    turning = rotation(positions)
    lane = lanes_of((TOK, 128))
    for head in range(HEADS_HERE):
        at = slice(head * TOK, (head + 1) * TOK)
        query_ref[at, :LATENT] = jnp.dot(
            joined[:, head * NOPE : (head + 1) * NOPE],
            key_up_ref[head],
            preferred_element_type=jnp.float32,
        ).astype(jnp.bfloat16)
        if head % 2 == 0:
            first = NOPES + head * ROPE
            turned = apply_rotation(joined[:, first : first + 128].astype(jnp.float32), *turning)
        else:
            turned = pltpu.roll(turned, ROPE, 1)
        query_ref[at, LATENT:] = jnp.where(lane < ROPE, turned, 0.0).astype(jnp.bfloat16)
        place_ref[at, :] = positions


def first_kernel(
    own_ref, key_up_ref, keys_ref, query_ref, place_ref, acc_ref, top_ref, sum_ref
):
    project(own_ref, key_up_ref, query_ref, place_ref)
    attend(query_ref, place_ref, [keys_ref], None, keep(acc_ref, top_ref, sum_ref))


def middle_kernel(keys_ref, *refs):
    for side in range(2):
        query_ref, place_ref, *old = refs[side * 5 : side * 5 + 5]
        new = refs[10 + side * 3 : 13 + side * 3]
        attend(query_ref, place_ref, [keys_ref], old, keep(*new))


def send_kernel(
    query_ref, place_ref, keys_ref, old_acc_ref, old_top_ref, old_sum_ref, out_ref
):
    def finish(start, product, top, total):
        at = start % ROWS
        whole = jnp.broadcast_to(jnp.sum(total, axis=1, keepdims=True), (CHUNK, 128))
        lane = lanes_of((CHUNK, 128))
        level = top + jnp.log2(whole)
        high = level.astype(jnp.bfloat16).astype(jnp.float32)
        rest = level - high
        middle = rest.astype(jnp.bfloat16).astype(jnp.float32)
        low = rest - middle
        pieces = jnp.where(
            lane == 0, high, jnp.where(lane == 1, middle, jnp.where(lane == 2, low, 0.0))
        )
        inverse = jnp.tile(1.0 / whole, (1, LATENT // 128))
        out_ref[at : at + CHUNK, :LATENT] = (product * inverse).astype(jnp.bfloat16)
        out_ref[at : at + CHUNK, LATENT:] = pieces.astype(jnp.bfloat16)

    old = (old_acc_ref, old_top_ref, old_sum_ref)
    attend(query_ref, place_ref, [keys_ref], old, finish)


def own_kernel(
    query_ref,
    place_ref,
    keys_ref,
    old_acc_ref,
    old_top_ref,
    old_sum_ref,
    acc_ref,
    top_ref,
    sum_ref,
):
    def finish(start, product, top, total):
        acc_ref[start : start + CHUNK, :] = product
        top_ref[start : start + CHUNK, :] = top
        sum_ref[start : start + CHUNK, :] = jnp.broadcast_to(
            jnp.sum(total, axis=1, keepdims=True), (CHUNK, 128)
        )

    old = (old_acc_ref, old_top_ref, old_sum_ref)
    attend(query_ref, place_ref, [keys_ref], old, finish)


def merge_kernel(acc_ref, top_ref, sum_ref, got_ref, value_up_ref, out_ref):
    for head in range(HEADS_HERE):
        at = slice(head * TOK, (head + 1) * TOK)
        level = jnp.sum(got_ref[at, LATENT:].astype(jnp.float32), axis=1, keepdims=True)
        level = jnp.broadcast_to(level, (TOK, 128))
        own_top = top_ref[at, :]
        top = jnp.maximum(own_top, level)
        one = jnp.exp2(own_top - top)
        two = jnp.exp2(level - top)
        inverse = 1.0 / (sum_ref[at, :] * one + two)
        one = jnp.tile(one * inverse, (1, LATENT // 128))
        two = jnp.tile(two * inverse, (1, LATENT // 128))
        latent = acc_ref[at, :] * one + got_ref[at, :LATENT].astype(jnp.float32) * two
        out_ref[:, head * VDIM : (head + 1) * VDIM] = jnp.dot(
            latent.astype(jnp.bfloat16), value_up_ref[head], preferred_element_type=jnp.float32
        ).astype(jnp.bfloat16)


def call(kernel, specs, out_shape, name, vmem=32, scratch=(), out_specs=None):
    out_specs = out_specs or jax.tree.map(lambda _: VMEM, out_shape)
    return pl.pallas_call(
        kernel,
        in_specs=specs,
        out_specs=out_specs,
        out_shape=out_shape,
        name=name,
        scratch_shapes=list(scratch),
        compiler_params=pltpu.CompilerParams(vmem_limit_bytes=vmem * 1024 * 1024),
    )


def device_at(y, z, x, c):
    y, z, x = y % NY, z % (NZH * NZL), x % NX
    return (((y * NZH + z // NZL) * NC + c) * NZL + z % NZL) * NX + x


def pairs(target):
    return [
        (device_at(y, z, x, c), device_at(*target(y, z, x, c)))
        for y in range(NY)
        for z in range(NZH * NZL)
        for x in range(NX)
        for c in range(NC)
    ]


def colours():
    return [
        [
            device_at(y, z, x, c)
            for y in range(NY)
            for z in range(NZH * NZL)
            for x in range(NX)
            if (x + y + 2 * z) % 4 == colour
        ]
        for colour in range(4)
        for c in range(NC)
    ]


def shards(query_nope, query_rope, compressed, latent_gain, key_up, value_up, span_order):
    f32 = jnp.float32
    bf16 = jnp.bfloat16
    shape = jax.ShapeDtypeStruct
    x_pairs = pairs(lambda y, z, x, c: (y, z, x - 1 + 2 * c, c))
    y_pairs = pairs(lambda y, z, x, c: (y + 1 - 2 * c, z, x, 1 - c))
    z_pairs = pairs(lambda y, z, x, c: (y, z - 1 + 2 * c, x, c))
    sibling_pairs = pairs(lambda y, z, x, c: (y, z, x, 1 - c))

    sent, joined = call(
        prep_kernel,
        [HBM] * 5,
        (shape((64, 8, WIDE), bf16), shape((TOK, JOINED), bf16)),
        "prep",
        60,
        [
            pltpu.SMEM((128,), jnp.int32),
            pltpu.VMEM((8, LATENT + ROPE), bf16),
            pltpu.VMEM((1, LATENT), f32),
            pltpu.SemaphoreType.DMA((5,)),
        ],
    )(span_order, compressed, latent_gain[None], query_nope, query_rope)
    own_keys = lax.all_to_all(
        sent, AXES, 0, 0, tiled=True, axis_index_groups=colours()
    ).reshape(512, WIDE)
    one = lax.ppermute(own_keys, AXES, x_pairs)
    two = lax.ppermute(own_keys, AXES, y_pairs)
    three = lax.ppermute(own_keys, AXES, z_pairs)
    sibling = lax.ppermute(joined, AXES, sibling_pairs)
    state = (shape((ROWS, LATENT), f32), shape((ROWS, 128), f32), shape((ROWS, 128), f32))
    rows = (shape((ROWS, WIDE), bf16), shape((ROWS, 128), f32))
    first = call(first_kernel, [VMEM] * 3, (*rows, *state), "first")
    here = first(joined, key_up, own_keys)
    there = first(sibling, key_up, own_keys)
    middle = call(middle_kernel, [VMEM] * 11, (*state, *state), "middle")
    carry = middle(two, *here, *there)
    carry = middle(one, *here[:2], *carry[:3], *there[:2], *carry[3:])
    send = call(send_kernel, [VMEM] * 6, shape((ROWS, WIDE), bf16), "sibling_rows")(
        *there[:2], three, *carry[3:]
    )
    got = lax.ppermute(send, AXES, sibling_pairs)
    own = call(own_kernel, [VMEM] * 6, state, "own_rows")(*here[:2], three, *carry[:3])
    return call(
        merge_kernel, [VMEM] * 5, shape((TOK, HEADS_HERE * VDIM), bf16), "merge", 16
    )(*own, got, value_up)


def solution(mesh):
    split = Mesh(mesh.devices.reshape(NY, NZH, NC, NZL, NX), AXES)
    placed = (
        P(BLK, HEAD),
        P(BLK, HEAD),
        P(AXES, None),
        P(),
        P(HEAD, None, None),
        P(HEAD, None, None),
        P(),
    )
    return jax.shard_map(
        shards, mesh=split, in_specs=placed, out_specs=P(BLK, HEAD), check_vma=False
    )
```

```python
import functools
import math

import jax
import jax.numpy as jnp
from jax import lax
from jax.experimental import pallas as pl
from jax.experimental.pallas import tpu as pltpu
from jax.sharding import Mesh
from jax.sharding import PartitionSpec as P

AXES = ("y", "zh", "c", "zl", "x")
BLK = ("y", "zh", "c")
HEAD = ("zl", "x")
NY, NZH, NC, NZL, NX = 8, 4, 2, 2, 4

LATENT = 512
ROPE = 64
NOPE = 128
VDIM = 128
HEADS_HERE = 8
TOK = 64
HALF = 32
WIDE = 640
ROWS = TOK * HEADS_HERE
NOPES = HEADS_HERE * NOPE
ROPES = HEADS_HERE * ROPE
JOINED = NOPES + ROPES + 128
CHUNK = 512

norm_epsilon = 1e-06
rope_base = 10000.0
masked_score = -1e30
score_scale = (NOPE + ROPE) ** (-0.5)
log2e = 1.4426950408889634

VMEM = pl.BlockSpec(memory_space=pltpu.VMEM)
SMEM = pl.BlockSpec(memory_space=pltpu.SMEM)
HBM = pl.BlockSpec(memory_space=pltpu.HBM)


def lanes_of(shape):
    return lax.broadcasted_iota(jnp.int32, shape, 1)


def rotation(positions):
    half = ROPE // 2
    lane = lanes_of(positions.shape)
    index = (lane % half).astype(jnp.float32)
    angles = positions * jnp.exp2(index * (-math.log2(rope_base) / half))
    leading = lane % ROPE < half
    sine_value = jnp.sin(angles)
    return jnp.cos(angles), jnp.where(leading, -sine_value, sine_value), leading


def apply_rotation(values, cosine, sine_value, leading):
    swapped = jnp.where(
        leading,
        pltpu.roll(values, 128 - ROPE // 2, 1),
        pltpu.roll(values, ROPE // 2, 1),
    )
    return values * cosine + swapped * sine_value


def block_index():
    return (lax.axis_index("y") * NZH + lax.axis_index("zh")) * NC + lax.axis_index("c")


def prep_kernel(
    span_hbm,
    compressed_hbm,
    gain_hbm,
    nope_hbm,
    rope_hbm,
    out_ref,
    joined_ref,
    span_ref,
    compressed_ref,
    gain_ref,
    sems,
):
    copies = [
        pltpu.make_async_copy(source, target, sems.at[k])
        for k, (source, target) in enumerate(
            (
                (compressed_hbm, compressed_ref),
                (gain_hbm, gain_ref),
                (span_hbm, span_ref),
            )
        )
    ]
    joins = [
        pltpu.make_async_copy(source, joined_ref.at[:, start : start + width], sems.at[3 + k])
        for k, (source, start, width) in enumerate(
            (
                (nope_hbm, 0, NOPES),
                (rope_hbm, NOPES, ROPES),
            )
        )
    ]
    for copy in copies + joins:
        copy.start()
    for copy in copies:
        copy.wait()
    rows = compressed_ref.shape[0]
    block = block_index()
    x = lax.axis_index("x")
    span = span_ref[block * 2 + lax.axis_index("zl")]
    offset = x * rows + lax.broadcasted_iota(jnp.int32, (rows, 128), 0)
    latent = compressed_ref[:, :LATENT].astype(jnp.float32)
    scale = lax.rsqrt(jnp.mean(latent * latent, axis=1, keepdims=True) + norm_epsilon)
    latent = (latent * scale * gain_ref[...]).astype(jnp.bfloat16)
    rope = compressed_ref[:, LATENT:].astype(jnp.float32)
    rope = jnp.concatenate([rope, jnp.zeros_like(rope)], axis=1)
    positions = (span * HALF + offset).astype(jnp.float32)
    turned = apply_rotation(rope, *rotation(positions))
    lane = lanes_of((rows, 128))
    tail = jnp.where(
        lane < ROPE,
        turned,
        jnp.where(
            lane == ROPE,
            span.astype(jnp.float32),
            jnp.where(lane == ROPE + 1, offset.astype(jnp.float32), 0.0),
        ),
    ).astype(jnp.bfloat16)
    row = jnp.concatenate([latent, tail], axis=1)
    out_ref[...] = jnp.broadcast_to(row[None], out_ref.shape)
    token = lax.broadcasted_iota(jnp.int32, (TOK, 128), 0)
    lane = lanes_of((TOK, 128))
    span = jnp.where(token < HALF, span_ref[block * 2], span_ref[block * 2 + 1])
    joined_ref[:, NOPES + ROPES :] = (
        jnp.where(lane == 0, span, jnp.where(lane == 1, token % HALF, 0))
        .astype(jnp.float32)
        .astype(jnp.bfloat16)
    )
    for copy in joins:
        copy.wait()


def position_rows():
    lane = lanes_of((16, WIDE))
    return jnp.where(
        lane == LATENT + ROPE, float(HALF), jnp.where(lane == LATENT + ROPE + 1, 1.0, 0.0)
    ).astype(jnp.bfloat16)


def query_positions(places):
    row = lax.broadcasted_iota(jnp.int32, (128, 128), 0)
    pick = jnp.where(row == 0, float(HALF), jnp.where(row == 1, 1.0, 0.0)).astype(jnp.bfloat16)
    return jnp.dot(places, pick, preferred_element_type=jnp.float32)


def attend(query_ref, place_ref, key_refs, carry, finish, rows=(0, ROWS)):
    keys = [ref[...] for ref in key_refs]
    places = [None] * len(keys)
    for start in range(*rows, CHUNK):
        queries = query_ref[start : start + CHUNK, :]
        if start == rows[0]:
            queries = jnp.concatenate([queries, position_rows()], axis=0)
        here = place_ref[start : start + CHUNK, :]
        scores = []
        for k, block in enumerate(keys):
            raw = lax.dot_general(
                queries, block, (((1,), (1,)), ((), ())), preferred_element_type=jnp.float32
            )
            if start == rows[0]:
                places[k] = raw[CHUNK : CHUNK + 8]
                raw = raw[:CHUNK]
            place = places[k]
            pieces = []
            for at in range(0, block.shape[0], 128):
                there = jnp.tile(place[:, at : at + 128], (CHUNK // 8, 1))
                pieces.append(
                    jnp.where(
                        there <= here, raw[:, at : at + 128] * (score_scale * log2e), masked_score
                    )
                )
            scores.append(pieces)
        top = functools.reduce(jnp.maximum, [piece for pieces in scores for piece in pieces])
        top = jnp.broadcast_to(jnp.max(top, axis=1, keepdims=True), (CHUNK, 128))
        if carry is not None:
            old_acc, old_top, old_sum = carry
            before = old_top[start : start + CHUNK, :]
            top = jnp.maximum(top, before)
        product = None
        total = None
        for block, pieces in zip(keys, scores):
            weights = [jnp.exp2(piece - top) for piece in pieces]
            for weight in weights:
                total = weight if total is None else total + weight
            term = jnp.dot(
                jnp.concatenate([weight.astype(jnp.bfloat16) for weight in weights], axis=1),
                block[:, :LATENT],
                preferred_element_type=jnp.float32,
            )
            product = term if product is None else product + term
        if carry is not None:
            shrink = jnp.exp2(before - top)
            product = product + old_acc[start : start + CHUNK, :] * jnp.tile(
                shrink, (1, LATENT // 128)
            )
            total = total + old_sum[start : start + CHUNK, :] * shrink
        finish(start, product, top, total)


def keep(acc_ref, top_ref, sum_ref):
    def finish(start, product, top, total):
        acc_ref[start : start + CHUNK, :] = product
        top_ref[start : start + CHUNK, :] = top
        sum_ref[start : start + CHUNK, :] = total

    return finish


def project(joined_ref, key_up_ref, query_ref, place_ref):
    joined = joined_ref[...]
    positions = query_positions(joined[:, NOPES + ROPES :])
    turning = rotation(positions)
    lane = lanes_of((TOK, 128))
    for head in range(HEADS_HERE):
        at = slice(head * TOK, (head + 1) * TOK)
        query_ref[at, :LATENT] = jnp.dot(
            joined[:, head * NOPE : (head + 1) * NOPE],
            key_up_ref[head],
            preferred_element_type=jnp.float32,
        ).astype(jnp.bfloat16)
        if head % 2 == 0:
            first = NOPES + head * ROPE
            turned = apply_rotation(joined[:, first : first + 128].astype(jnp.float32), *turning)
        else:
            turned = pltpu.roll(turned, ROPE, 1)
        query_ref[at, LATENT:] = jnp.where(lane < ROPE, turned, 0.0).astype(jnp.bfloat16)
        place_ref[at, :] = positions


def first_kernel(
    own_ref, key_up_ref, keys_ref, query_ref, place_ref, acc_ref, top_ref, sum_ref
):
    project(own_ref, key_up_ref, query_ref, place_ref)
    attend(query_ref, place_ref, [keys_ref], None, keep(acc_ref, top_ref, sum_ref))


def middle_kernel(keys_ref, *refs):
    for side in range(2):
        query_ref, place_ref, *old = refs[side * 5 : side * 5 + 5]
        new = refs[10 + side * 3 : 13 + side * 3]
        attend(query_ref, place_ref, [keys_ref], old, keep(*new))


def send_kernel(
    query_ref, place_ref, keys_ref, old_acc_ref, old_top_ref, old_sum_ref, out_ref
):
    def finish(start, product, top, total):
        at = start % ROWS
        whole = jnp.broadcast_to(jnp.sum(total, axis=1, keepdims=True), (CHUNK, 128))
        lane = lanes_of((CHUNK, 128))
        level = top + jnp.log2(whole)
        high = level.astype(jnp.bfloat16).astype(jnp.float32)
        rest = level - high
        middle = rest.astype(jnp.bfloat16).astype(jnp.float32)
        low = rest - middle
        pieces = jnp.where(
            lane == 0, high, jnp.where(lane == 1, middle, jnp.where(lane == 2, low, 0.0))
        )
        inverse = jnp.tile(1.0 / whole, (1, LATENT // 128))
        out_ref[at : at + CHUNK, :LATENT] = (product * inverse).astype(jnp.bfloat16)
        out_ref[at : at + CHUNK, LATENT:] = pieces.astype(jnp.bfloat16)

    old = (old_acc_ref, old_top_ref, old_sum_ref)
    attend(query_ref, place_ref, [keys_ref], old, finish)


def own_kernel(
    query_ref,
    place_ref,
    keys_ref,
    old_acc_ref,
    old_top_ref,
    old_sum_ref,
    acc_ref,
    top_ref,
    sum_ref,
):
    def finish(start, product, top, total):
        acc_ref[start : start + CHUNK, :] = product
        top_ref[start : start + CHUNK, :] = top
        sum_ref[start : start + CHUNK, :] = jnp.broadcast_to(
            jnp.sum(total, axis=1, keepdims=True), (CHUNK, 128)
        )

    old = (old_acc_ref, old_top_ref, old_sum_ref)
    attend(query_ref, place_ref, [keys_ref], old, finish)


def merge_kernel(acc_ref, top_ref, sum_ref, got_ref, value_up_ref, out_ref):
    for head in range(HEADS_HERE):
        at = slice(head * TOK, (head + 1) * TOK)
        level = jnp.sum(got_ref[at, LATENT:].astype(jnp.float32), axis=1, keepdims=True)
        level = jnp.broadcast_to(level, (TOK, 128))
        own_top = top_ref[at, :]
        top = jnp.maximum(own_top, level)
        one = jnp.exp2(own_top - top)
        two = jnp.exp2(level - top)
        inverse = 1.0 / (sum_ref[at, :] * one + two)
        one = jnp.tile(one * inverse, (1, LATENT // 128))
        two = jnp.tile(two * inverse, (1, LATENT // 128))
        latent = acc_ref[at, :] * one + got_ref[at, :LATENT].astype(jnp.float32) * two
        out_ref[:, head * VDIM : (head + 1) * VDIM] = jnp.dot(
            latent.astype(jnp.bfloat16), value_up_ref[head], preferred_element_type=jnp.float32
        ).astype(jnp.bfloat16)


def call(kernel, specs, out_shape, name, vmem=32, scratch=(), out_specs=None):
    out_specs = out_specs or jax.tree.map(lambda _: VMEM, out_shape)
    return pl.pallas_call(
        kernel,
        in_specs=specs,
        out_specs=out_specs,
        out_shape=out_shape,
        name=name,
        scratch_shapes=list(scratch),
        compiler_params=pltpu.CompilerParams(vmem_limit_bytes=vmem * 1024 * 1024),
    )


def device_at(y, z, x, c):
    y, z, x = y % NY, z % (NZH * NZL), x % NX
    return (((y * NZH + z // NZL) * NC + c) * NZL + z % NZL) * NX + x


def pairs(target):
    return [
        (device_at(y, z, x, c), device_at(*target(y, z, x, c)))
        for y in range(NY)
        for z in range(NZH * NZL)
        for x in range(NX)
        for c in range(NC)
    ]


def colours():
    return [
        [
            device_at(y, z, x, c)
            for y in range(NY)
            for z in range(NZH * NZL)
            for x in range(NX)
            if (x + y + 2 * z) % 4 == colour
        ]
        for colour in range(4)
        for c in range(NC)
    ]


def shards(query_nope, query_rope, compressed, latent_gain, key_up, value_up, span_order):
    f32 = jnp.float32
    bf16 = jnp.bfloat16
    shape = jax.ShapeDtypeStruct
    x_pairs = pairs(lambda y, z, x, c: (y, z, x - 1 + 2 * c, c))
    y_pairs = pairs(lambda y, z, x, c: (y + 1 - 2 * c, z, x, 1 - c))
    z_pairs = pairs(lambda y, z, x, c: (y, z - 1 + 2 * c, x, c))
    sibling_pairs = pairs(lambda y, z, x, c: (y, z, x, 1 - c))

    sent, joined = call(
        prep_kernel,
        [HBM] * 5,
        (shape((64, 8, WIDE), bf16), shape((TOK, JOINED), bf16)),
        "prep",
        60,
        [
            pltpu.SMEM((128,), jnp.int32),
            pltpu.VMEM((8, LATENT + ROPE), bf16),
            pltpu.VMEM((1, LATENT), f32),
            pltpu.SemaphoreType.DMA((5,)),
        ],
    )(span_order, compressed, latent_gain[None], query_nope, query_rope)
    own_keys = lax.all_to_all(
        sent, AXES, 0, 0, tiled=True, axis_index_groups=colours()
    ).reshape(512, WIDE)
    one = lax.ppermute(own_keys, AXES, z_pairs)
    two = lax.ppermute(own_keys, AXES, y_pairs)
    three = lax.ppermute(own_keys, AXES, x_pairs)
    sibling = lax.ppermute(joined, AXES, sibling_pairs)
    state = (shape((ROWS, LATENT), f32), shape((ROWS, 128), f32), shape((ROWS, 128), f32))
    rows = (shape((ROWS, WIDE), bf16), shape((ROWS, 128), f32))
    first = call(first_kernel, [VMEM] * 3, (*rows, *state), "first")
    here = first(joined, key_up, own_keys)
    there = first(sibling, key_up, own_keys)
    middle = call(middle_kernel, [VMEM] * 11, (*state, *state), "middle")
    carry = middle(two, *here, *there)
    carry = middle(one, *here[:2], *carry[:3], *there[:2], *carry[3:])
    send = call(send_kernel, [VMEM] * 6, shape((ROWS, WIDE), bf16), "sibling_rows")(
        *there[:2], three, *carry[3:]
    )
    got = lax.ppermute(send, AXES, sibling_pairs)
    own = call(own_kernel, [VMEM] * 6, state, "own_rows")(*here[:2], three, *carry[:3])
    return call(
        merge_kernel, [VMEM] * 5, shape((TOK, HEADS_HERE * VDIM), bf16), "merge", 16
    )(*own, got, value_up)


def solution(mesh):
    split = Mesh(mesh.devices.reshape(NY, NZH, NC, NZL, NX), AXES)
    placed = (
        P(BLK, HEAD),
        P(BLK, HEAD),
        P(AXES, None),
        P(),
        P(HEAD, None, None),
        P(HEAD, None, None),
        P(),
    )
    return jax.shard_map(
        shards, mesh=split, in_specs=placed, out_specs=P(BLK, HEAD), check_vma=False
    )
```
